256 devices in a mesh: ctx: 32 (over z, x_hi, core), pipe: 8 (over y, x_lo).
Axes of the slice: x: 4 (x_hi: 2, x_lo: 2; x = x_hi * 2 + x_lo), y: 4, z: 8, core: 2. Of those that a mesh axis runs over, the one named last changes fastest.
Arguments:
- query_fwd: bfloat16 [8, 4096, 2048], P('pipe', 'ctx'), may hold values from -6 to 6
- key_fwd: bfloat16 [8, 4096, 512], P('pipe', 'ctx'), may hold values from -6 to 6
- value_fwd: bfloat16 [8, 4096, 512], P('pipe', 'ctx'), may hold values from -6 to 6
- gate_fwd: bfloat16 [8, 4096, 2048], P('pipe', 'ctx'), may hold values from -6 to 6
- types_fwd: int32 [8, 4096], P('pipe', 'ctx'), may hold values from 0 to 63
- query_bwd: bfloat16 [8, 4096, 2048], P('pipe', 'ctx'), may hold values from -6 to 6
- key_bwd: bfloat16 [8, 4096, 512], P('pipe', 'ctx'), may hold values from -6 to 6
- value_bwd: bfloat16 [8, 4096, 512], P('pipe', 'ctx'), may hold values from -6 to 6
- grad_out: bfloat16 [8, 4096, 2048], P('pipe', 'ctx'), may hold values from -6 to 6
- types_bwd: int32 [8, 4096], P('pipe', 'ctx'), may hold values from 0 to 63
- type_key: bfloat16 [8, 64, 512], P('pipe'), may hold values from -4.1875 to 4.1875
- norm_gain: float32 [8, 2048], P('pipe'), may hold values from 0.5 to 1.5
- stretch_order: int32 [8, 64], P('pipe'), may hold values from 0 to 63, as said below
Outputs:
- handed: bfloat16 [8, 4096, 2048], P('pipe', 'ctx')
- query_grad: bfloat16 [8, 4096, 2048], P('pipe', 'ctx')
- key_grad: bfloat16 [8, 4096, 512], P('pipe', 'ctx')
- value_grad: bfloat16 [8, 4096, 512], P('pipe', 'ctx')
The draws below stay inside these ranges and needn't reach their ends.
Inputs may be any that keep to these rules, and one draw needn't show every extreme that they name: `stretch_order`: in each section's row the stored stretch slots 2 c and 2 c + 1 (those of index c of ctx) hold two stretches whose numbers add to 63, in either order; each row names every stretch once.
All inputs are finite; a program needn't handle non-finite values.
Results may differ from the reference program's by a relative error of at most 0.02.
Values may be sent and summed in bfloat16 or wider, within the bound.
A program may use at most 128 MiB of HBM per device.

```python
import math
import jax
import jax.numpy as jnp
from jax import lax

HEAD = 128
TYPES = 64
TOK_DEV = 128
STRETCHES = 64
TOKENS = 4096
SECTIONS = 8
QW = 2048
KVW = 512
N_CTX = 32


def draw_stretch_order(key, part):
    key = jax.random.fold_in(key, 11)
    section_keys = jax.random.split(key, SECTIONS)

    def one_section(section_key):
        perm_key, flip_key = jax.random.split(section_key)
        early_ids = jax.random.permutation(perm_key, STRETCHES // 2).astype(jnp.int32)
        late_ids = STRETCHES - 1 - early_ids
        flip_bits = jax.random.randint(flip_key, (STRETCHES // 2,), 0, 2, dtype=jnp.int32)
        leading = jnp.where(flip_bits == 1, late_ids, early_ids)
        trailing = jnp.where(flip_bits == 1, early_ids, late_ids)
        return jnp.stack([leading, trailing], axis=1).reshape(STRETCHES).astype(jnp.int32)
    return jax.vmap(one_section)(section_keys)


def with_ends(result, rng, smallest, largest):
    longest = result.shape.index(max(result.shape))
    spots = []
    for shift in (0, 1):
        where = [jax.random.randint(jax.random.fold_in(rng, axis), (), 0, length) for axis, length in enumerate(result.shape)]
        where[longest] = (where[longest] + shift) % result.shape[longest]
        spots.append(tuple(where))
    return result.at[spots[0]].set(smallest).at[spots[1]].set(largest)


def level_of(rng, extent, cuts, least, largest):
    gain = 1.0
    for dim, blocks in cuts:
        heights = jax.random.uniform(jax.random.fold_in(jax.random.fold_in(rng, 6), dim), (blocks,), jnp.float32, least / len(cuts), largest / len(cuts))
        gain = gain * jnp.repeat(jnp.exp(heights), extent[dim] // blocks).reshape((-1,) + (1,) * (len(extent) - 1 - dim))
    return gain


def normal_values(rng, shape, spread, most, cuts=(), kind=jnp.bfloat16):
    array = spread * jax.random.normal(rng, shape, jnp.float32)
    if cuts:
        array = array * level_of(rng, shape, cuts, -0.22, 0.18)
    return jnp.clip(array, -most, most).astype(kind)


def setup_inputs(seed: int = 0) -> dict:
    key_list = jax.random.split(jax.random.key(seed), 14)
    return {
        "query_fwd": normal_values(key_list[0], (SECTIONS, TOKENS, QW), 1.0, 6.0, ((0, 8), (1, 32))),
        "key_fwd": normal_values(key_list[1], (SECTIONS, TOKENS, KVW), 1.0, 6.0, ((0, 8), (1, 32))),
        "value_fwd": normal_values(key_list[2], (SECTIONS, TOKENS, KVW), 1.0, 6.0, ((0, 8), (1, 32))),
        "gate_fwd": normal_values(key_list[3], (SECTIONS, TOKENS, QW), 1.0, 6.0, ((0, 8), (1, 32))),
        "types_fwd": with_ends(jax.random.randint(key_list[4], (SECTIONS, TOKENS), 0, TYPES), jax.random.fold_in(key_list[4], 1), 0, TYPES - 1).astype(jnp.int32),
        "query_bwd": normal_values(key_list[5], (SECTIONS, TOKENS, QW), 1.0, 6.0, ((0, 8), (1, 32))),
        "key_bwd": normal_values(key_list[6], (SECTIONS, TOKENS, KVW), 1.0, 6.0, ((0, 8), (1, 32))),
        "value_bwd": normal_values(key_list[7], (SECTIONS, TOKENS, KVW), 1.0, 6.0, ((0, 8), (1, 32))),
        "grad_out": normal_values(key_list[8], (SECTIONS, TOKENS, QW), 1.0, 6.0, ((0, 8), (1, 32))),
        "types_bwd": with_ends(jax.random.randint(key_list[9], (SECTIONS, TOKENS), 0, TYPES), jax.random.fold_in(key_list[9], 1), 0, TYPES - 1).astype(jnp.int32),
        "type_key": normal_values(key_list[10], (SECTIONS, TYPES, KVW), 0.7, 4.1875, ((0, 8),)),
        "norm_gain": jnp.clip(1.0 + 0.1 * jax.random.normal(key_list[11], (SECTIONS, QW), jnp.float32), 0.5, 1.5),
        "stretch_order": draw_stretch_order(jax.random.fold_in(key_list[13], 71), 0),
    }


norm_eps = 1e-06

def silu_slope(scores):
    sigmoid_part = jax.nn.sigmoid(scores)
    return sigmoid_part * (1.0 + scores * (1.0 - sigmoid_part))

def typed_keys(key_rows, event_types, type_table):
    onehot = (event_types[:, None] == jnp.arange(type_table.shape[0], dtype=jnp.int32)[None, :]).astype(jnp.bfloat16)
    type_rows = jnp.dot(onehot, type_table, preferred_element_type=jnp.float32)
    return (key_rows.astype(jnp.float32) + type_rows).astype(jnp.bfloat16)

def invert(stretch_perm):
    total_stretches = stretch_perm.shape[0]
    matches = stretch_perm[None, :] == jnp.arange(total_stretches, dtype=jnp.int32)[:, None]
    return lax.optimization_barrier(jnp.sum(jnp.where(matches, jnp.arange(total_stretches, dtype=jnp.int32)[None, :], 0), axis=1)).astype(jnp.int32)

def to_sequence(stored, inverse, stretch_rows):
    return jnp.take(stored.reshape(-1, stretch_rows, stored.shape[1]), inverse, axis=0).reshape(-1, stored.shape[1])

def position(stretch_perm, slot_index, stretch_rows):
    leading = lax.dynamic_index_in_dim(stretch_perm, slot_index, keepdims=False)
    return leading * stretch_rows + jnp.arange(stretch_rows, dtype=jnp.int32)

def score_block(queries, query_pos, key_rows, value_rows, key_pos):
    row_count = queries.shape[0]
    kv_heads = key_rows.shape[1] // HEAD
    groups = queries.shape[1] // key_rows.shape[1]
    query_heads = queries.astype(jnp.float32).reshape(row_count, kv_heads, groups, HEAD)
    key_heads = key_rows.astype(jnp.float32).reshape(-1, kv_heads, HEAD)
    value_heads = value_rows.astype(jnp.float32).reshape(-1, kv_heads, HEAD)
    scores = jnp.einsum('qhgd,thd->hgqt', query_heads, key_heads) * HEAD ** (-0.5)
    visible = key_pos[None, :] <= query_pos[:, None]
    shrink = lax.rsqrt((query_pos + 1).astype(jnp.float32))[:, None]
    weights = (jnp.where(visible, jax.nn.silu(scores), 0.0) * shrink).astype(jnp.bfloat16)
    return (query_heads, key_heads, value_heads, scores, visible, shrink, weights)

def forward_block(queries, query_pos, key_rows, value_rows, key_pos):
    query_heads, key_heads, value_heads, scores, visible, shrink, weights = score_block(queries, query_pos, key_rows, value_rows, key_pos)
    return jnp.einsum('hgqt,thd->qhgd', weights.astype(jnp.float32), value_heads).reshape(queries.shape[0], -1)

def backward_block(queries, grad_rows, query_pos, key_rows, value_rows, key_pos):
    query_heads, key_heads, value_heads, scores, visible, shrink, weights = score_block(queries, query_pos, key_rows, value_rows, key_pos)
    grad_heads = grad_rows.astype(jnp.float32).reshape(query_heads.shape)
    weight_grad = jnp.einsum('qhgd,thd->hgqt', grad_heads, value_heads)
    score_grad = (jnp.where(visible, weight_grad * silu_slope(scores), 0.0) * shrink).astype(jnp.bfloat16)
    query_part = jnp.einsum('hgqt,thd->qhgd', score_grad.astype(jnp.float32), key_heads).reshape(queries.shape[0], -1)
    key_part = jnp.einsum('hgqt,qhgd->thd', score_grad.astype(jnp.float32), query_heads) * HEAD ** (-0.5)
    value_part = jnp.einsum('hgqt,qhgd->thd', weights.astype(jnp.float32), grad_heads)
    kv_width = key_rows.shape[1]
    return (query_part, jnp.concatenate([key_part.reshape(-1, kv_width), value_part.reshape(-1, kv_width)], axis=1))

def rows_forward(queries, query_pos, seq_keys, seq_values, block_rows):
    block_count = query_pos[-1] // block_rows + 1

    def advance(step_index, running):
        offset = step_index * block_rows
        key_rows = lax.dynamic_slice_in_dim(seq_keys, offset, block_rows, 0)
        value_rows = lax.dynamic_slice_in_dim(seq_values, offset, block_rows, 0)
        key_pos = offset + jnp.arange(block_rows, dtype=jnp.int32)
        return running + forward_block(queries, query_pos, key_rows, value_rows, key_pos)
    return lax.fori_loop(0, block_count, advance, jnp.zeros(queries.shape, jnp.float32))

def rows_backward(queries, grad_rows, query_pos, seq_keys, seq_values, block_rows, buffer):
    block_count = query_pos[-1] // block_rows + 1

    def advance(step_index, carried):
        running, buffer_in = carried
        offset = step_index * block_rows
        key_rows = lax.dynamic_slice_in_dim(seq_keys, offset, block_rows, 0)
        value_rows = lax.dynamic_slice_in_dim(seq_values, offset, block_rows, 0)
        key_pos = offset + jnp.arange(block_rows, dtype=jnp.int32)
        query_part, kv_part = backward_block(queries, grad_rows, query_pos, key_rows, value_rows, key_pos)
        former = lax.dynamic_slice_in_dim(buffer_in, offset, block_rows, 0)
        return (running + query_part, lax.dynamic_update_slice_in_dim(buffer_in, former + kv_part, offset, 0))
    return lax.fori_loop(0, block_count, advance, (jnp.zeros(queries.shape, jnp.float32), buffer))

def one_section(inputs):
    query_fwd, key_fwd, value_fwd, gate_fwd, types_fwd, query_bwd, key_bwd, value_bwd, grad_out, types_bwd, type_table, norm_gain, stretch_perm = inputs
    stretch_rows = TOK_DEV // 2
    block_rows = math.gcd(TOKENS, 512)
    kv_width = key_fwd.shape[1]
    inverse = invert(stretch_perm)
    keys_f = typed_keys(key_fwd, types_fwd, type_table)
    keys_b = typed_keys(key_bwd, types_bwd, type_table)
    seq_keys_f = to_sequence(keys_f, inverse, stretch_rows)
    seq_values_f = to_sequence(value_fwd, inverse, stretch_rows)
    seq_keys_b = to_sequence(keys_b, inverse, stretch_rows)
    seq_values_b = to_sequence(value_bwd, inverse, stretch_rows)

    def forward_device(device):
        outputs = []
        for stretch_slot in range(2):
            slot_index = 2 * device + stretch_slot
            queries = lax.dynamic_slice_in_dim(query_fwd, slot_index * stretch_rows, stretch_rows, 0)
            outputs.append(rows_forward(queries, position(stretch_perm, slot_index, stretch_rows), seq_keys_f, seq_values_f, block_rows))
        return jnp.concatenate(outputs, axis=0)
    attended = lax.map(forward_device, jnp.arange(N_CTX, dtype=jnp.int32)).reshape(TOKENS, -1)
    mean_square = lax.optimization_barrier(jnp.mean(attended * attended, axis=1, keepdims=True))
    gated = (attended * lax.rsqrt(mean_square + norm_eps) * norm_gain[None, :] * gate_fwd.astype(jnp.float32)).astype(jnp.bfloat16)

    def backward_device(grand_total, device):
        buffer = jnp.zeros((TOKENS, 2 * kv_width), jnp.float32)
        query_parts = []
        for stretch_slot in range(2):
            slot_index = 2 * device + stretch_slot
            queries = lax.dynamic_slice_in_dim(query_bwd, slot_index * stretch_rows, stretch_rows, 0)
            grad_rows = lax.dynamic_slice_in_dim(grad_out, slot_index * stretch_rows, stretch_rows, 0)
            query_part, buffer = rows_backward(queries, grad_rows, position(stretch_perm, slot_index, stretch_rows), seq_keys_b, seq_values_b, block_rows, buffer)
            query_parts.append(query_part)
        rounded = lax.optimization_barrier(buffer.astype(jnp.bfloat16))
        return (grand_total + rounded.astype(jnp.float32), jnp.concatenate(query_parts, axis=0))
    grand_total, query_sums = lax.scan(backward_device, jnp.zeros((TOKENS, 2 * kv_width), jnp.float32), jnp.arange(N_CTX, dtype=jnp.int32))
    query_grad = (query_sums.reshape(TOKENS, -1) * HEAD ** (-0.5)).astype(jnp.bfloat16)
    stored = jnp.take(grand_total.reshape(-1, stretch_rows, 2 * kv_width), stretch_perm, axis=0).reshape(TOKENS, 2 * kv_width)
    return (gated, query_grad, stored[:, :kv_width].astype(jnp.bfloat16), stored[:, kv_width:].astype(jnp.bfloat16))

def reference(query_fwd, key_fwd, value_fwd, gate_fwd, types_fwd, query_bwd, key_bwd, value_bwd, grad_out, types_bwd, type_key, norm_gain, stretch_order):
    gated, query_grad, key_grad, value_grad = lax.map(one_section, (query_fwd, key_fwd, value_fwd, gate_fwd, types_fwd, query_bwd, key_bwd, value_bwd, grad_out, types_bwd, type_key, norm_gain, stretch_order))
    handed = jnp.roll(gated, 1, axis=0)
    return (handed, query_grad, key_grad, value_grad)
```

```python
import functools

import jax
import jax.numpy as jnp
from jax import lax
from jax.experimental import pallas as pl
from jax.experimental.pallas import tpu as pltpu
from jax.sharding import PartitionSpec as P

HEAD = 128
ROWS = 128
HALF = 64
GROUP = 4
RING = 8
CTX = GROUP * RING
TOKENS = CTX * ROWS
BLOCK = 256
EPS = 1e-06
SCALE = HEAD**-0.5
BF = jnp.bfloat16
F32 = jnp.float32
MESH = pl.DeviceIdType.MESH
VMEM = pl.BlockSpec(memory_space=pltpu.VMEM)
ANY = pl.BlockSpec(memory_space=pl.ANY)


def place():
    me = lax.axis_index("ctx")
    z = me // GROUP
    m = me % GROUP
    x, c = m // 2, m % 2
    peers = (2 * x + (1 - c), 2 * (1 - x) + c, 2 * (1 - x) + (1 - c))
    return z, m, peers


def ctx_of(z, m):
    return {"ctx": ((z + RING) % RING) * GROUP + m}


def remote(src, dst, send, recv, target):
    return pltpu.make_async_remote_copy(
        src_ref=src,
        dst_ref=dst,
        send_sem=send,
        recv_sem=recv,
        device_id=target,
        device_id_type=MESH,
    )


def greet(targets):
    barrier = pltpu.get_barrier_semaphore()
    for target in targets:
        pl.semaphore_signal(barrier, inc=1, device_id=target, device_id_type=MESH)
    return lambda: pl.semaphore_wait(barrier, len(targets))


def gather_kernel(
    types_f, types_b, table, qf, kf, vf, qb, kb, vb, go,
    out_q, out_f, out_b,
    stage_q, stage_kv, local_sem, a_send, a_recv, r_send, r_recv,
):
    z, m, peers = place()
    greeted = greet(
        [ctx_of(z, p) for p in peers] + [ctx_of(z + 1, m), ctx_of(z - 1, m)]
    )
    outs = (out_f, out_b)
    for t, (types, keys, values) in enumerate(((types_f, kf, vf), (types_b, kb, vb))):
        kinds = lax.broadcasted_iota(jnp.int32, (table.shape[0], ROWS), 0)
        onehot = jnp.where(kinds == types[...], 1.0, 0.0).astype(BF)
        rows = lax.dot_general(
            onehot, table[...], (((0,), (0,)), ((), ())), preferred_element_type=F32
        )
        typed = (keys[...].astype(F32) + rows).astype(BF)
        for h in range(GROUP):
            stage_kv[t, h, 0] = typed[:, h * HEAD : (h + 1) * HEAD]
            stage_kv[t, h, 1] = values[:, h * HEAD : (h + 1) * HEAD]
    greeted()
    started = []
    arrivals_kv = []
    for t in range(2):
        arriving = []
        for d, p in enumerate(peers):
            copy = remote(
                stage_kv.at[t, p], outs[t].at[z * GROUP + m],
                a_send.at[d, t], a_recv.at[d, t], ctx_of(z, p),
            )
            copy.start()
            arriving.append(copy)
            started.append(copy)
        arrivals_kv.append(arriving)
    own = []
    for t in range(2):
        copy = pltpu.make_async_copy(
            stage_kv.at[t, m], outs[t].at[z * GROUP + m], local_sem.at[t]
        )
        copy.start()
        own.append(copy)
    arrivals_q = []
    for t, source in enumerate((qf, qb, go)):
        for h in range(GROUP):
            for g in range(4):
                col = (h * 4 + g) * HEAD
                stage_q[t, h, g] = source[:, col : col + HEAD]
        for d, p in enumerate(peers):
            copy = remote(
                stage_q.at[t, p], out_q.at[t, m],
                a_send.at[d, 2 + t], a_recv.at[d, 2 + t], ctx_of(z, p),
            )
            copy.start()
            arrivals_q.append(copy)
            started.append(copy)
        copy = pltpu.make_async_copy(
            stage_q.at[t, m], out_q.at[t, m], local_sem.at[2 + t]
        )
        copy.start()
        own.append(copy)

    def hop(t, step, way):
        chunk = ((z - way * (step - 1) + RING) % RING) * GROUP
        first, count = (0, GROUP) if step < RING // 2 else ((1 - way), 2)
        part = outs[t].at[pl.ds(chunk + first, count)]
        lane = 0 if way == 1 else 1
        copy = remote(
            part, part, r_send.at[t, lane, step - 1], r_recv.at[t, lane, step - 1],
            ctx_of(z + way, m),
        )
        copy.start()
        started.append(copy)
        return copy

    moving = {}
    for t in range(2):
        own[t].wait()
        for copy in arrivals_kv[t]:
            copy.wait_recv()
        for way in (1, -1):
            moving[t, way] = hop(t, 1, way)
    for step in range(2, RING // 2 + 1):
        for t in range(2):
            for way in (1, -1):
                moving[t, way].wait_recv()
                moving[t, way] = hop(t, step, way)
    for t in range(2):
        for way in (1, -1):
            moving[t, way].wait_recv()
    for copy in arrivals_q:
        copy.wait_recv()
    for copy in started:
        copy.wait_send()
    for copy in own[2:]:
        copy.wait()


def dot_nt(a, b):
    return lax.dot_general(a, b, (((1,), (1,)), ((), ())), preferred_element_type=F32)


def dot_nn(a, b):
    return jnp.dot(a, b, preferred_element_type=F32)


def attention_kernel(
    order, q_all, kv_f, kv_b, att, dq, dkv,
    ks, vs, kt, dk, dv, acc, acc_t,
):
    z = lax.axis_index("ctx") // GROUP

    def unsort(kv):
        def fill(j, _):
            for half in range(2):
                at = pl.ds(pl.multiple_of(order[2 * j + half] * HALF, HALF), HALF)
                ks[at, :] = kv[j, 0, half * HALF : (half + 1) * HALF]
                vs[at, :] = kv[j, 1, half * HALF : (half + 1) * HALF]
            return 0

        lax.fori_loop(0, CTX, fill, 0)

    def shrink_rows(stretch):
        row = lax.broadcasted_iota(jnp.int32, (4 * HALF, HEAD), 0) % HALF
        return lax.rsqrt((stretch * HALF + row + 1).astype(F32))

    unsort(kv_f)

    def forward(i, _):
        s, half = i // 2, i % 2
        stretch = order[2 * GROUP * z + i]
        rows = pl.ds(pl.multiple_of(half * HALF, HALF), HALF)
        q = q_all[0, s, :, rows, :].reshape(4 * HALF, HEAD)
        acc[...] = jnp.zeros_like(acc)

        def step(b, masked):
            at = pl.ds(pl.multiple_of(b * BLOCK, BLOCK), BLOCK)
            u = dot_nt(q, ks[at, :]) * (0.5 * SCALE)
            w = u + u * jnp.tanh(u)
            if masked:
                row = lax.broadcasted_iota(jnp.int32, w.shape, 0) % HALF
                col = lax.broadcasted_iota(jnp.int32, w.shape, 1)
                w = jnp.where(col + b * BLOCK <= row + stretch * HALF, w, 0.0)
            acc[...] += dot_nn(w.astype(BF), vs[at, :])

        full = stretch * HALF // BLOCK

        def loop(b, _):
            step(b, False)
            return 0

        lax.fori_loop(0, full, loop, 0)
        step(full, True)
        att[s, :, rows, :] = (
            (acc[...] * shrink_rows(stretch)).astype(BF).reshape(4, HALF, HEAD)
        )
        return 0

    lax.fori_loop(0, 2 * GROUP, forward, 0)

    unsort(kv_b)

    def turn(b, _):
        at = pl.ds(pl.multiple_of(b * BLOCK, BLOCK), BLOCK)
        kt[:, at] = ks[at, :].T
        dk[at, :] = jnp.zeros((BLOCK, HEAD), F32)
        dv[at, :] = jnp.zeros((BLOCK, HEAD), F32)
        return 0

    lax.fori_loop(0, TOKENS // BLOCK, turn, 0)

    def backward(i, _):
        s, half = i // 2, i % 2
        stretch = order[2 * GROUP * z + i]
        rows = pl.ds(pl.multiple_of(half * HALF, HALF), HALF)
        q = q_all[1, s, :, rows, :].reshape(4 * HALF, HEAD)
        g = q_all[2, s, :, rows, :].reshape(4 * HALF, HEAD)
        g = (g.astype(F32) * shrink_rows(stretch)).astype(BF)
        acc_t[...] = jnp.zeros_like(acc_t)

        def step(b, masked):
            at = pl.ds(pl.multiple_of(b * BLOCK, BLOCK), BLOCK)
            u = dot_nt(ks[at, :], q) * (0.5 * SCALE)
            grad = dot_nt(vs[at, :], g)
            t = jnp.tanh(u)
            ut = u * t
            w = u + ut
            slope = (0.5 + 0.5 * t) * (1.0 + (u - ut)) * grad
            if masked:
                row = lax.broadcasted_iota(jnp.int32, w.shape, 0)
                col = lax.broadcasted_iota(jnp.int32, w.shape, 1) % HALF
                seen = row + b * BLOCK <= col + stretch * HALF
                w = jnp.where(seen, w, 0.0)
                slope = jnp.where(seen, slope, 0.0)
            w = w.astype(BF)
            slope = slope.astype(BF)
            dv[at, :] += dot_nn(w, g)
            dk[at, :] += dot_nn(slope, q)
            acc_t[...] += dot_nn(kt[:, at], slope)

        full = stretch * HALF // BLOCK

        def loop(b, _):
            step(b, False)
            return 0

        lax.fori_loop(0, full, loop, 0)
        step(full, True)
        dq[s, :, rows, :] = (
            (acc_t[...] * SCALE).T.astype(BF).reshape(4, HALF, HEAD)
        )
        return 0

    lax.fori_loop(0, 2 * GROUP, backward, 0)

    def store(j, _):
        for half in range(2):
            at = pl.ds(pl.multiple_of(order[2 * j + half] * HALF, HALF), HALF)
            dkv[j, 0, half * HALF : (half + 1) * HALF] = (dk[at, :] * SCALE).astype(BF)
            dkv[j, 1, half * HALF : (half + 1) * HALF] = dv[at, :].astype(BF)
        return 0

    lax.fori_loop(0, CTX, store, 0)


def scatter_kernel(
    dkv, att, dq, gate, gain,
    handed, query_grad, key_grad, value_grad,
    sums, landed, total, att_in, dq_in, dkv_in, gated,
    r_send, r_recv, a_send, a_recv, h_send, h_recv,
):
    z, m, peers = place()
    sections = lax.axis_size("pipe")
    after = {"pipe": (lax.axis_index("pipe") + 1) % sections}
    before = {"pipe": (lax.axis_index("pipe") + sections - 1) % sections}
    greet(
        [ctx_of(z, p) for p in peers]
        + [ctx_of(z + 1, m), ctx_of(z - 1, m), after, before]
    )()
    started = []

    def exchange(t, source, target):
        copies = []
        for d, p in enumerate(peers):
            copy = remote(
                source.at[p], target.at[m], a_send.at[d, t], a_recv.at[d, t], ctx_of(z, p)
            )
            copy.start()
            copies.append(copy)
            started.append(copy)
        return copies

    def hop(step, way, part):
        chunk = ((z + way * (RING // 2 - step) + RING) % RING) * GROUP
        lane = 0 if way == 1 else 1
        mine = pl.ds(chunk + 2 * part, 2)
        if step == 0 or (step == 1 and part != lane):
            source = dkv.at[mine]
        else:
            arrived = landed[lane, step - 1, part].astype(F32)
            sums[lane, step - 1, part] = (dkv[mine].astype(F32) + arrived).astype(BF)
            source = sums.at[lane, step - 1, part]
        copy = remote(
            source, landed.at[lane, step, part],
            r_send.at[lane, step, part], r_recv.at[lane, step, part], ctx_of(z + way, m),
        )
        copy.start()
        started.append(copy)
        return copy

    att_copies = exchange(0, att, att_in)
    moving = {}
    for way, part in ((1, 0), (-1, 1)):
        moving[way, part] = hop(0, way, part)
    for way, part in ((1, 1), (-1, 0)):
        moving[way, part] = hop(1, way, part)
    for way, part in ((1, 0), (-1, 1)):
        moving[way, part].wait_recv()
        moving[way, part] = hop(1, way, part)
    dq_copies = exchange(1, dq, dq_in)

    for copy in att_copies:
        copy.wait_recv()
    att_in[m] = att[m]
    squares = jnp.zeros((ROWS, HEAD), F32)
    for h in range(GROUP):
        for g in range(4):
            part = att_in[h, g].astype(F32)
            squares += part * part
    mean = jnp.sum(squares, axis=1, keepdims=True) * (1.0 / (16 * HEAD))
    factor = lax.rsqrt(mean + EPS)
    for h in range(GROUP):
        for g in range(4):
            cols = slice((h * 4 + g) * HEAD, (h * 4 + g + 1) * HEAD)
            gated[:, cols] = (
                att_in[h, g].astype(F32) * factor * gain[:, cols] * gate[:, cols].astype(F32)
            ).astype(BF)
    hand = remote(gated, handed, h_send, h_recv, after)
    hand.start()

    for step in (2, 3):
        for part in range(2):
            for way in (1, -1):
                moving[way, part].wait_recv()
                moving[way, part] = hop(step, way, part)

    for copy in dq_copies:
        copy.wait_recv()
    dq_in[m] = dq[m]
    for h in range(GROUP):
        for g in range(4):
            cols = slice((h * 4 + g) * HEAD, (h * 4 + g + 1) * HEAD)
            query_grad[:, cols] = dq_in[h, g]

    for part in range(2):
        for way in (1, -1):
            moving[way, part].wait_recv()
        mine = pl.ds(z * GROUP + 2 * part, 2)
        total[2 * part : 2 * part + 2] = (
            dkv[mine].astype(F32)
            + landed[0, RING // 2 - 1, part].astype(F32)
            + landed[1, RING // 2 - 1, part].astype(F32)
        ).astype(BF)
    kv_copies = exchange(2, total, dkv_in)
    dkv_in[m] = total[m]
    for copy in kv_copies:
        copy.wait_recv()
    for h in range(GROUP):
        cols = slice(h * HEAD, (h + 1) * HEAD)
        key_grad[:, cols] = dkv_in[h, 0]
        value_grad[:, cols] = dkv_in[h, 1]
    for copy in started:
        copy.wait_send()
    hand.wait()


def body(
    query_fwd, key_fwd, value_fwd, gate_fwd, types_fwd,
    query_bwd, key_bwd, value_bwd, grad_out, types_bwd,
    type_key, norm_gain, stretch_order,
):
    dma, tile = pltpu.SemaphoreType.DMA, (HEAD, HEAD)
    params = functools.partial(
        pltpu.CompilerParams, vmem_limit_bytes=56 * 1024 * 1024
    )
    q_all, kv_f, kv_b = pl.pallas_call(
        gather_kernel,
        out_shape=(
            jax.ShapeDtypeStruct((3, GROUP, 4, *tile), BF),
            jax.ShapeDtypeStruct((CTX, 2, *tile), BF),
            jax.ShapeDtypeStruct((CTX, 2, *tile), BF),
        ),
        in_specs=[VMEM] * 10,
        out_specs=(ANY, ANY, ANY),
        scratch_shapes=[
            pltpu.VMEM((3, GROUP, 4, *tile), BF),
            pltpu.VMEM((2, GROUP, 2, *tile), BF),
            dma((5,)),
            dma((3, 5)),
            dma((3, 5)),
            dma((2, 2, RING // 2)),
            dma((2, 2, RING // 2)),
        ],
        compiler_params=params(collective_id=0, has_side_effects=True),
        name="gather",
    )(
        types_fwd, types_bwd, type_key[0], query_fwd[0], key_fwd[0], value_fwd[0],
        query_bwd[0], key_bwd[0], value_bwd[0], grad_out[0],
    )
    att, dq, dkv = pl.pallas_call(
        attention_kernel,
        out_shape=(
            jax.ShapeDtypeStruct((GROUP, 4, *tile), BF),
            jax.ShapeDtypeStruct((GROUP, 4, *tile), BF),
            jax.ShapeDtypeStruct((CTX, 2, *tile), BF),
        ),
        in_specs=[pl.BlockSpec(memory_space=pltpu.SMEM), VMEM, VMEM, VMEM],
        out_specs=(VMEM, VMEM, VMEM),
        scratch_shapes=[
            pltpu.VMEM((TOKENS, HEAD), BF),
            pltpu.VMEM((TOKENS, HEAD), BF),
            pltpu.VMEM((HEAD, TOKENS), BF),
            pltpu.VMEM((TOKENS, HEAD), F32),
            pltpu.VMEM((TOKENS, HEAD), F32),
            pltpu.VMEM((4 * HALF, HEAD), F32),
            pltpu.VMEM((HEAD, 4 * HALF), F32),
        ],
        compiler_params=params(),
        name="attention",
    )(stretch_order[0], q_all, kv_f, kv_b)
    wide, narrow = (ROWS, 16 * HEAD), (ROWS, GROUP * HEAD)
    handed, query_grad, key_grad, value_grad = pl.pallas_call(
        scatter_kernel,
        out_shape=(
            jax.ShapeDtypeStruct(wide, BF),
            jax.ShapeDtypeStruct(wide, BF),
            jax.ShapeDtypeStruct(narrow, BF),
            jax.ShapeDtypeStruct(narrow, BF),
        ),
        in_specs=[VMEM] * 5,
        out_specs=(ANY, VMEM, VMEM, VMEM),
        scratch_shapes=[
            pltpu.VMEM((2, RING // 2 - 1, 2, 2, 2, *tile), BF),
            pltpu.VMEM((2, RING // 2, 2, 2, 2, *tile), BF),
            pltpu.VMEM((GROUP, 2, *tile), BF),
            pltpu.VMEM((GROUP, 4, *tile), BF),
            pltpu.VMEM((GROUP, 4, *tile), BF),
            pltpu.VMEM((GROUP, 2, *tile), BF),
            pltpu.VMEM(wide, BF),
            dma((2, RING // 2, 2)),
            dma((2, RING // 2, 2)),
            dma((3, 3)),
            dma((3, 3)),
            dma,
            dma,
        ],
        compiler_params=params(collective_id=1, has_side_effects=True),
        name="scatter",
    )(dkv, att, dq, gate_fwd[0], norm_gain)
    return handed[None], query_grad[None], key_grad[None], value_grad[None]


def solution(mesh):
    rows = P("pipe", "ctx", None)
    section = P("pipe", None)
    types = P("pipe", "ctx")
    return jax.shard_map(
        body,
        mesh=mesh,
        in_specs=(
            rows, rows, rows, rows, types, rows, rows, rows, rows, types,
            P("pipe", None, None), section, section,
        ),
        out_specs=(rows, rows, rows, rows),
        check_vma=False,
    )
```

```python
import jax
import jax.numpy as jnp
from jax import lax
from jax.experimental import pallas as pl
from jax.experimental.pallas import tpu as pltpu
from jax.sharding import PartitionSpec as P

HEAD = 128
ROWS = 128
HALF = 64
GROUP = 4
RING = 8
CTX = GROUP * RING
TOKENS = CTX * ROWS
QROWS = 4 * HALF
BLOCK = 256
EPS = 1e-06
SCALE = HEAD**-0.5
BF = jnp.bfloat16
F32 = jnp.float32
MESH = pl.DeviceIdType.MESH
VMEM = pl.BlockSpec(memory_space=pltpu.VMEM)
ANY = pl.BlockSpec(memory_space=pl.ANY)


def place():
    me = lax.axis_index("ctx")
    z = me // GROUP
    m = me % GROUP
    x, c = m // 2, m % 2
    peers = (2 * x + (1 - c), 2 * (1 - x) + c, 2 * (1 - x) + (1 - c))
    return z, m, peers


def ctx_of(z, m):
    return {"ctx": ((z + RING) % RING) * GROUP + m}


def remote(src, dst, send, recv, target):
    return pltpu.make_async_remote_copy(
        src_ref=src,
        dst_ref=dst,
        send_sem=send,
        recv_sem=recv,
        device_id=target,
        device_id_type=MESH,
    )


def greet(targets):
    barrier = pltpu.get_barrier_semaphore()
    for target in targets:
        pl.semaphore_signal(barrier, inc=1, device_id=target, device_id_type=MESH)
    return lambda: pl.semaphore_wait(barrier, len(targets))


def dot_nt(a, b):
    return lax.dot_general(a, b, (((1,), (1,)), ((), ())), preferred_element_type=F32)


def dot_nn(a, b):
    return jnp.dot(a, b, preferred_element_type=F32)


def stretches(b):
    return pl.ds(b * (BLOCK // HALF), BLOCK // HALF)


def columns(i):
    return slice(i * HEAD, (i + 1) * HEAD)


def kernel(
    order, inverse, types_f, types_b, table, qf, kf, vf, qb, kb, vb, go, gate, gain,
    handed, query_grad, key_grad, value_grad,
    stage_q, stage_kv, in_qf, in_qb, in_go, in_kvf, in_kvb,
    ks, vs, kt, dk, dv, acc, acc_t, qs, gs, dgk, dgv, q_pick, g_pick,
    dkv, sums, landed, total, dkv_in, att, att_in, dq, dq_in, gated,
    a_send, a_recv, g_send, g_recv, r_send, r_recv, h_send, h_recv,
):
    z, m, peers = place()
    sections = lax.axis_size("pipe")
    after = {"pipe": (lax.axis_index("pipe") + 1) % sections}
    before = {"pipe": (lax.axis_index("pipe") + sections - 1) % sections}
    greeted = greet(
        [ctx_of(z, p) for p in peers]
        + [ctx_of(z + 1, m), ctx_of(z - 1, m), after, before]
    )
    started = []


    def exchange(t, source, target, slot):
        copies = []
        for d, p in enumerate(peers):
            copy = remote(
                source.at[p], target.at[slot], a_send.at[d, t], a_recv.at[d, t], ctx_of(z, p)
            )
            copy.start()
            copies.append(copy)
            started.append(copy)
        return copies

    def stage_keys(t, types, keys, values):
        kinds = lax.broadcasted_iota(jnp.int32, (table.shape[0], ROWS), 0)
        onehot = jnp.where(kinds == types[...], 1.0, 0.0).astype(BF)
        rows = lax.dot_general(
            onehot, table[...], (((0,), (0,)), ((), ())), preferred_element_type=F32
        )
        typed = (keys[...].astype(F32) + rows).astype(BF)
        for h in range(GROUP):
            for half in range(2):
                rows = slice(half * HALF, (half + 1) * HALF)
                stage_kv[t, h, 0, half] = typed[rows, columns(h)]
                stage_kv[t, h, 1, half] = values[rows, columns(h)]

    def stage_rows(t, source):
        for h in range(GROUP):
            for g in range(4):
                for half in range(2):
                    rows = slice(half * HALF, (half + 1) * HALF)
                    stage_q[t, h, half, g] = source[rows, columns(h * 4 + g)]

    stage_keys(1, types_b, kb, vb)
    greeted()
    kvb_copies = exchange(0, stage_kv.at[1], in_kvb, z * GROUP + m)
    in_kvb[z * GROUP + m] = stage_kv[1, m]
    stage_rows(1, qb)
    qb_copies = exchange(1, stage_q.at[1], in_qb, m)
    in_qb[m] = stage_q[1, m]
    stage_rows(2, go)
    go_copies = exchange(2, stage_q.at[2], in_go, m)
    in_go[m] = stage_q[2, m]
    stage_keys(0, types_f, kf, vf)
    kvf_copies = exchange(3, stage_kv.at[0], in_kvf, z * GROUP + m)
    in_kvf[z * GROUP + m] = stage_kv[0, m]
    stage_rows(0, qf)
    qf_copies = exchange(4, stage_q.at[0], in_qf, m)
    in_qf[m] = stage_q[0, m]

    def arrive(copies):
        for copy in copies:
            copy.wait_recv()


    moving = {}

    def spread(t, step):
        target = (in_kvf, in_kvb)[t]
        for lane, way in enumerate((1, -1)):
            if step > 1:
                moving[t, lane].wait_recv()
            chunk = ((z - way * (step - 1) + RING) % RING) * GROUP
            first, count = (0, GROUP) if step < RING // 2 else (2 * lane, 2)
            part = target.at[pl.ds(chunk + first, count)]
            copy = remote(
                part, part, g_send.at[t, lane, step - 1], g_recv.at[t, lane, step - 1],
                ctx_of(z + way, m),
            )
            copy.start()
            started.append(copy)
            moving[t, lane] = copy

    def gathered(t):
        for lane in range(2):
            moving[t, lane].wait_recv()

    arrive(kvb_copies)
    for step in range(1, RING // 2 + 1):
        spread(1, step)
    arrive(kvf_copies)
    spread(0, 1)
    gathered(1)
    arrive(qb_copies)
    arrive(go_copies)


    first = [order[2 * GROUP * z + 2 * i] for i in range(GROUP)]
    second = [order[2 * GROUP * z + 2 * i + 1] for i in range(GROUP)]
    low = [jnp.minimum(a, b) for a, b in zip(first, second)]
    low_half = [jnp.where(a < b, 0, 1) for a, b in zip(first, second)]
    quart = [a * HALF // BLOCK for a in low]
    last = TOKENS // BLOCK - 1
    stretch = [low, [2 * CTX - 1 - a for a in low]]
    span = [slice(i * QROWS, (i + 1) * QROWS) for i in range(GROUP)]
    row_in = lax.broadcasted_iota(jnp.int32, (QROWS, HEAD), 0) % HALF

    def shrink_rows(position):
        return lax.rsqrt((position * HALF + row_in + 1).astype(F32))

    def query_rows(source, i, w):
        half = low_half[i] if w == 0 else 1 - low_half[i]
        return source[i, half].reshape(QROWS, HEAD)

    def choice(i, n):
        is_low = n <= quart[i]
        return is_low, jnp.where(is_low, n, last - n), jnp.where(is_low, 0, 1)

    def bound_low(i, n):
        return jnp.where(n == quart[i], low[i] * HALF - n * BLOCK, BLOCK)

    def bound_high(i):
        return stretch[1][i] * HALF - (last - quart[i]) * BLOCK

    def put_rows(target, i, low_rows, high_rows):
        shape = (4, HALF, HEAD)
        a, b = low_rows.astype(BF).reshape(shape), high_rows.astype(BF).reshape(shape)
        target[i, 0] = jnp.where(low_half[i] == 0, a, b)
        target[i, 1] = jnp.where(low_half[i] == 0, b, a)

    def unsort(source):
        def fill(b, _):
            for k in range(BLOCK // HALF):
                j = inverse[b * (BLOCK // HALF) + k]
                ks[b, k * HALF : (k + 1) * HALF] = source[j // 2, 0, j % 2]
                vs[b, k * HALF : (k + 1) * HALF] = source[j // 2, 1, j % 2]
            return 0

        lax.fori_loop(0, last + 1, fill, 0)


    unsort(in_kvb)

    def turn(b, _):
        kt[b] = ks[b].T
        return 0

    lax.fori_loop(0, last + 1, turn, 0)
    for i in range(GROUP):
        for w in range(2):
            qs[w, i] = query_rows(in_qb, i, w)
            g = query_rows(in_go, i, w).astype(F32) * shrink_rows(stretch[w][i])
            gs[w, i] = g.astype(BF)
    key_over = lax.broadcasted_iota(jnp.int32, (BLOCK, QROWS), 0) - (
        lax.broadcasted_iota(jnp.int32, (BLOCK, QROWS), 1) % HALF
    )

    def slopes(k, v, q, g):
        u = dot_nt(k, q) * (0.5 * SCALE)
        grad = dot_nt(v, g)
        t = jnp.tanh(u)
        ut = u * t
        return u + ut, (0.5 + 0.5 * t) * (1.0 + (u - ut)) * grad

    def seen(over, bound, value):
        return jnp.where(over <= bound, value, 0.0).astype(BF)

    def backward_full(b, _):
        q, g = qs[1].reshape(GROUP * QROWS, HEAD), gs[1].reshape(GROUP * QROWS, HEAD)
        p, s = slopes(ks[b], vs[b], q, g)
        p = p.astype(BF)
        s = s.astype(BF)
        dv[stretches(b)] = dot_nn(p, g).reshape(-1, HALF, HEAD)
        dk[stretches(b)] = dot_nn(s, q).reshape(-1, HALF, HEAD)
        acc_t[1] += dot_nn(kt[b], s)
        return 0

    def backward_edge(i):
        at = last - quart[i]
        q, g = qs[1, i], gs[1, i]
        p, s = slopes(ks[at], vs[at], q, g)
        p = seen(key_over, bound_high(i), p)
        s = seen(key_over, bound_high(i), s)
        dgv[i] = dot_nn(p, g)
        dgk[i] = dot_nn(s, q)
        acc_t[1, :, span[i]] += dot_nn(kt[at], s)

    def backward_choice(n, _):
        zero = jnp.zeros((QROWS, HEAD), BF)
        ps, ss = [], []
        for i in range(GROUP):
            is_low, at, w = choice(i, n)
            q, g = qs[w, i], gs[w, i]
            p, s = slopes(ks[at], vs[at], q, g)
            p = seen(key_over, bound_low(i, n), p)
            s = seen(key_over, bound_low(i, n), s)
            part = dot_nn(kt[at], s)
            acc_t[0, :, span[i]] += jnp.where(is_low, part, 0.0)
            acc_t[1, :, span[i]] += jnp.where(is_low, 0.0, part)
            g_pick[span[i], :HEAD] = jnp.where(is_low, g, zero)
            g_pick[span[i], HEAD:] = jnp.where(is_low, zero, g)
            q_pick[span[i], :HEAD] = jnp.where(is_low, q, zero)
            q_pick[span[i], HEAD:] = jnp.where(is_low, zero, q)
            ps.append(p)
            ss.append(s)
        both_v = dot_nn(jnp.concatenate(ps, 1), g_pick[...])
        both_k = dot_nn(jnp.concatenate(ss, 1), q_pick[...])
        dv[stretches(n)] += both_v[:, :HEAD].reshape(-1, HALF, HEAD)
        dk[stretches(n)] += both_k[:, :HEAD].reshape(-1, HALF, HEAD)
        high_v, high_k = both_v[:, HEAD:], both_k[:, HEAD:]
        for i in range(GROUP):
            here = jnp.where(n == quart[i], 1.0, 0.0)
            high_v += dgv[i] * here
            high_k += dgk[i] * here
        dv[stretches(last - n)] = high_v.reshape(-1, HALF, HEAD)
        dk[stretches(last - n)] = high_k.reshape(-1, HALF, HEAD)
        return 0

    half_blocks = (last + 1) // 2
    middle = half_blocks // 2
    acc_t[...] = jnp.zeros_like(acc_t)
    lax.fori_loop(0, middle, backward_full, 0)
    spread(0, 2)
    lax.fori_loop(middle, half_blocks, backward_full, 0)
    for i in range(GROUP):
        backward_edge(i)
    spread(0, 3)
    lax.fori_loop(0, middle, backward_choice, 0)
    spread(0, 4)
    lax.fori_loop(middle, half_blocks, backward_choice, 0)


    def store_chunk(distance):
        chunk = ((z + distance + RING) % RING) * GROUP

        def store(c, _):
            for half in range(2):
                p = order[2 * (chunk + c) + half]
                dkv[chunk + c, 0, half] = (dk[p] * SCALE).astype(BF)
                dkv[chunk + c, 1, half] = dv[p].astype(BF)
            return 0

        lax.fori_loop(0, GROUP, store, 0)

    reducing = {}

    def reduce(step, lane, part):
        way = (1, -1)[lane]
        chunk = ((z + way * (RING // 2 - step) + RING) % RING) * GROUP
        mine = pl.ds(chunk + 2 * part, 2)
        if step == 0 or (step == 1 and part != lane):
            source = dkv.at[mine]
        else:
            reducing[lane, part].wait_recv()
            arrived = landed[lane, step - 1, part].astype(F32)
            sums[lane, step - 1, part] = (dkv[mine].astype(F32) + arrived).astype(BF)
            source = sums.at[lane, step - 1, part]
        copy = remote(
            source, landed.at[lane, step, part],
            r_send.at[lane, step, part], r_recv.at[lane, step, part], ctx_of(z + way, m),
        )
        copy.start()
        started.append(copy)
        reducing[lane, part] = copy

    def reduce_all(step):
        for part in range(2):
            for lane in range(2):
                reduce(step, lane, part)

    store_chunk(RING // 2)
    for lane in range(2):
        reduce(0, lane, lane)
    for distance in (3, -3):
        store_chunk(distance)
    for lane in range(2):
        reduce(1, lane, 1 - lane)
    for i in range(GROUP):
        put_rows(
            dq, i, (acc_t[0, :, span[i]] * SCALE).T, (acc_t[1, :, span[i]] * SCALE).T
        )
    dq_copies = exchange(5, dq, dq_in, m)
    dq_in[m] = dq[m]
    for distance in (2, -2, 1, -1, 0):
        store_chunk(distance)


    gathered(0)
    arrive(qf_copies)
    unsort(in_kvf)
    for i in range(GROUP):
        for w in range(2):
            qs[w, i] = query_rows(in_qf, i, w)
    query_over = lax.broadcasted_iota(jnp.int32, (QROWS, BLOCK), 1) - (
        lax.broadcasted_iota(jnp.int32, (QROWS, BLOCK), 0) % HALF
    )

    def weigh(q, k):
        u = dot_nt(q, k) * (0.5 * SCALE)
        return u + u * jnp.tanh(u)

    def forward_full(b, _):
        q = qs[1].reshape(GROUP * QROWS, HEAD)
        acc[1] += dot_nn(weigh(q, ks[b]).astype(BF), vs[b])
        return 0

    def forward_choice(n, _):
        for i in range(GROUP):
            is_low, at, w = choice(i, n)
            p = seen(query_over, bound_low(i, n), weigh(qs[w, i], ks[at]))
            part = dot_nn(p, vs[at])
            acc[0, span[i]] += jnp.where(is_low, part, 0.0)
            acc[1, span[i]] += jnp.where(is_low, 0.0, part)
        return 0

    acc[...] = jnp.zeros_like(acc)
    lax.fori_loop(0, middle, forward_full, 0)
    for lane in range(2):
        reduce(1, lane, lane)
    lax.fori_loop(middle, half_blocks, forward_full, 0)
    for i in range(GROUP):
        at = last - quart[i]
        p = seen(query_over, bound_high(i), weigh(qs[1, i], ks[at]))
        acc[1, span[i]] += dot_nn(p, vs[at])
    lax.fori_loop(0, middle, forward_choice, 0)
    reduce_all(2)
    lax.fori_loop(middle, half_blocks, forward_choice, 0)
    for i in range(GROUP):
        put_rows(
            att, i,
            acc[0, span[i]] * shrink_rows(stretch[0][i]),
            acc[1, span[i]] * shrink_rows(stretch[1][i]),
        )
    att_copies = exchange(6, att, att_in, m)
    att_in[m] = att[m]
    reduce_all(3)


    arrive(att_copies)
    for half in range(2):
        rows = slice(half * HALF, (half + 1) * HALF)
        squares = jnp.zeros((HALF, HEAD), F32)
        for h in range(GROUP):
            for g in range(4):
                part = att_in[h, half, g].astype(F32)
                squares += part * part
        mean = jnp.sum(squares, axis=1, keepdims=True) * (1.0 / (16 * HEAD))
        factor = lax.rsqrt(mean + EPS)
        for h in range(GROUP):
            for g in range(4):
                cols = columns(h * 4 + g)
                gated[rows, cols] = (
                    att_in[h, half, g].astype(F32)
                    * factor * gain[:, cols] * gate[rows, cols].astype(F32)
                ).astype(BF)
    hand = remote(gated, handed, h_send, h_recv, after)
    hand.start()

    arrive(dq_copies)
    for h in range(GROUP):
        for g in range(4):
            for half in range(2):
                rows = slice(half * HALF, (half + 1) * HALF)
                query_grad[rows, columns(h * 4 + g)] = dq_in[h, half, g]
    for part in range(2):
        for lane in range(2):
            reducing[lane, part].wait_recv()
        mine = pl.ds(z * GROUP + 2 * part, 2)
        total[2 * part : 2 * part + 2] = (
            dkv[mine].astype(F32)
            + landed[0, RING // 2 - 1, part].astype(F32)
            + landed[1, RING // 2 - 1, part].astype(F32)
        ).astype(BF)
    kv_copies = exchange(7, total, dkv_in, m)
    dkv_in[m] = total[m]
    arrive(kv_copies)
    for h in range(GROUP):
        for half in range(2):
            rows = slice(half * HALF, (half + 1) * HALF)
            key_grad[rows, columns(h)] = dkv_in[h, 0, half]
            value_grad[rows, columns(h)] = dkv_in[h, 1, half]
    for copy in started:
        copy.wait_send()
    hand.wait()


def body(
    query_fwd, key_fwd, value_fwd, gate_fwd, types_fwd,
    query_bwd, key_bwd, value_bwd, grad_out, types_bwd,
    type_key, norm_gain, stretch_order,
):
    order = stretch_order[0]
    slots = jnp.arange(order.shape[0], dtype=jnp.int32)
    inverse = jnp.sum(
        jnp.where(order[None, :] == slots[:, None], slots[None, :], 0), axis=1
    ).astype(jnp.int32)
    dma = pltpu.SemaphoreType.DMA
    wide, narrow = (ROWS, 16 * HEAD), (ROWS, GROUP * HEAD)
    smem = pl.BlockSpec(memory_space=pltpu.SMEM)
    part = (HALF, HEAD)
    blocks = TOKENS // BLOCK
    heads, pairs = (GROUP, 2, 4, *part), (CTX, 2, 2, *part)
    handed, query_grad, key_grad, value_grad = pl.pallas_call(
        kernel,
        out_shape=(
            jax.ShapeDtypeStruct(wide, BF),
            jax.ShapeDtypeStruct(wide, BF),
            jax.ShapeDtypeStruct(narrow, BF),
            jax.ShapeDtypeStruct(narrow, BF),
        ),
        in_specs=[smem, smem] + [VMEM] * 12,
        out_specs=(ANY, VMEM, VMEM, VMEM),
        scratch_shapes=[
            pltpu.VMEM((3, *heads), BF),
            pltpu.VMEM((2, GROUP, 2, 2, *part), BF),
            pltpu.VMEM(heads, BF),
            pltpu.VMEM(heads, BF),
            pltpu.VMEM(heads, BF),
            pltpu.VMEM(pairs, BF),
            pltpu.VMEM(pairs, BF),
            pltpu.VMEM((blocks, BLOCK, HEAD), BF),
            pltpu.VMEM((blocks, BLOCK, HEAD), BF),
            pltpu.VMEM((blocks, HEAD, BLOCK), BF),
            pltpu.VMEM((2 * CTX, *part), F32),
            pltpu.VMEM((2 * CTX, *part), F32),
            pltpu.VMEM((2, GROUP * QROWS, HEAD), F32),
            pltpu.VMEM((2, HEAD, GROUP * QROWS), F32),
            pltpu.VMEM((2, GROUP, QROWS, HEAD), BF),
            pltpu.VMEM((2, GROUP, QROWS, HEAD), BF),
            pltpu.VMEM((GROUP, BLOCK, HEAD), F32),
            pltpu.VMEM((GROUP, BLOCK, HEAD), F32),
            pltpu.VMEM((GROUP * QROWS, 2 * HEAD), BF),
            pltpu.VMEM((GROUP * QROWS, 2 * HEAD), BF),
            pltpu.VMEM(pairs, BF),
            pltpu.VMEM((2, RING // 2 - 1, 2, 2, 2, 2, *part), BF),
            pltpu.VMEM((2, RING // 2, 2, 2, 2, 2, *part), BF),
            pltpu.VMEM((GROUP, 2, 2, *part), BF),
            pltpu.VMEM((GROUP, 2, 2, *part), BF),
            pltpu.VMEM(heads, BF),
            pltpu.VMEM(heads, BF),
            pltpu.VMEM(heads, BF),
            pltpu.VMEM(heads, BF),
            pltpu.VMEM(wide, BF),
            dma((3, 8)),
            dma((3, 8)),
            dma((2, 2, RING // 2)),
            dma((2, 2, RING // 2)),
            dma((2, RING // 2, 2)),
            dma((2, RING // 2, 2)),
            dma,
            dma,
        ],
        compiler_params=pltpu.CompilerParams(
            collective_id=0, has_side_effects=True, vmem_limit_bytes=56 * 1024 * 1024
        ),
        name="attention",
    )(
        order, inverse, types_fwd, types_bwd, type_key[0],
        query_fwd[0], key_fwd[0], value_fwd[0],
        query_bwd[0], key_bwd[0], value_bwd[0], grad_out[0], gate_fwd[0], norm_gain,
    )
    return handed[None], query_grad[None], key_grad[None], value_grad[None]


def solution(mesh):
    rows = P("pipe", "ctx", None)
    section = P("pipe", None)
    types = P("pipe", "ctx")
    return jax.shard_map(
        body,
        mesh=mesh,
        in_specs=(
            rows, rows, rows, rows, types, rows, rows, rows, rows, types,
            P("pipe", None, None), section, section,
        ),
        out_specs=(rows, rows, rows, rows),
        check_vma=False,
    )
```

```python
import jax
import jax.numpy as jnp
from jax import lax
from jax.experimental import pallas as pl
from jax.experimental.pallas import tpu as pltpu
from jax.sharding import PartitionSpec as P

HEAD = 128
ROWS = 128
HALF = 64
GROUP = 4
RING = 8
CTX = GROUP * RING
TOKENS = CTX * ROWS
QROWS = 4 * HALF
BLOCK = 256
EPS = 1e-06
SCALE = HEAD**-0.5
BF = jnp.bfloat16
F32 = jnp.float32
MESH = pl.DeviceIdType.MESH
VMEM = pl.BlockSpec(memory_space=pltpu.VMEM)


def place():
    me = lax.axis_index("ctx")
    z = me // GROUP
    m = me % GROUP
    x, c = m // 2, m % 2
    peers = (2 * x + (1 - c), 2 * (1 - x) + c, 2 * (1 - x) + (1 - c))
    return z, m, peers


def ctx_of(z, m):
    return {"ctx": ((z + RING) % RING) * GROUP + m}


def remote(src, dst, send, recv, target):
    return pltpu.make_async_remote_copy(
        src_ref=src,
        dst_ref=dst,
        send_sem=send,
        recv_sem=recv,
        device_id=target,
        device_id_type=MESH,
    )


def greet(targets):
    barrier = pltpu.get_barrier_semaphore()
    for target in targets:
        pl.semaphore_signal(barrier, inc=1, device_id=target, device_id_type=MESH)
    return lambda: pl.semaphore_wait(barrier, len(targets))


def dot_nt(a, b):
    return lax.dot_general(a, b, (((1,), (1,)), ((), ())), preferred_element_type=F32)


def dot_nn(a, b):
    return jnp.dot(a, b, preferred_element_type=F32)


def stretches(b):
    return pl.ds(b * (BLOCK // HALF), BLOCK // HALF)


def columns(i):
    return slice(i * HEAD, (i + 1) * HEAD)


def kernel(
    order, types_f, types_b, table, qf, kf, vf, qb, kb, vb, go, gate, gain,
    handed, query_grad, key_grad, value_grad,
    inverse, stage_q, stage_kv, in_qf, in_qb, in_go, in_gate, in_kvf, in_kvb,
    ks, vs, kt, dk, dv, acc, acc_t, qs, gs, dgk, dgv, q_pick, g_pick,
    dkv, sums, landed, total, dkv_in, att, norms, norms_in, dq, dq_in, gated, hand_in,
    a_send, a_recv, b_send, b_recv, g_send, g_recv, r_send, r_recv,
    n_send, n_recv, h_send, h_recv,
):
    z, m, peers = place()
    x = m // 2
    members = (m, *peers)
    chips = (2 * x, 2 * (1 - x))
    sections = lax.axis_size("pipe")
    section = lax.axis_index("pipe")

    def beside(distance, member):
        return {
            "pipe": (section + distance + sections) % sections,
            "ctx": z * GROUP + member,
        }

    greeted = greet(
        [ctx_of(z, p) for p in peers]
        + [ctx_of(z + 1, m), ctx_of(z - 1, m)]
        + [beside(d, s) for d in (1, -1) for s in range(GROUP)]
    )
    started = []


    def exchange(t, source, target, slot):
        copies = []
        for d, p in enumerate(peers):
            copy = remote(
                source.at[p], target.at[slot], a_send.at[d, t], a_recv.at[d, t], ctx_of(z, p)
            )
            copy.start()
            copies.append(copy)
            started.append(copy)
        return copies

    def stage_keys(t, types, keys, values):
        kinds = lax.broadcasted_iota(jnp.int32, (table.shape[0], ROWS), 0)
        onehot = jnp.where(kinds == types[...], 1.0, 0.0).astype(BF)
        rows = lax.dot_general(
            onehot, table[...], (((0,), (0,)), ((), ())), preferred_element_type=F32
        )
        typed = (keys[...].astype(F32) + rows).astype(BF)
        for h in range(GROUP):
            for half in range(2):
                rows = slice(half * HALF, (half + 1) * HALF)
                stage_kv[t, h, 0, half] = typed[rows, columns(h)]
                stage_kv[t, h, 1, half] = values[rows, columns(h)]

    def stage_rows(t, source):
        for h in range(GROUP):
            for g in range(4):
                for half in range(2):
                    rows = slice(half * HALF, (half + 1) * HALF)
                    stage_q[t, h, half, g] = source[rows, columns(h * 4 + g)]

    def arrive(copies):
        for copy in copies:
            copy.wait_recv()


    moving = {}

    def ring_hop(t, target, first, count, step, lane, part, send, recv):
        way = (1, -1)[lane]
        if step > 1:
            moving[t, lane, part].wait_recv()
        chunk = ((z - way * (step - 1) + RING) % RING) * GROUP
        view = target.at[pl.ds(chunk + first, count)]
        copy = remote(
            view, view, send.at[lane, step - 1, part], recv.at[lane, step - 1, part],
            ctx_of(z + way, m),
        )
        copy.start()
        started.append(copy)
        moving[t, lane, part] = copy

    def spread_b(step, d):
        for lane in range(2):
            if step < RING // 2 or d % 2 == lane:
                ring_hop(1, in_kvb, members[d], 1, step, lane, d, b_send, b_recv)

    def spread_f(step, part):
        for lane in range(2):
            if step < RING // 2 or part == lane:
                ring_hop(0, in_kvf, chips[part], 2, step, lane, part, g_send, g_recv)

    def gathered(t):
        for (kind, _, _), copy in moving.items():
            if kind == t:
                copy.wait_recv()

    def invert(first, count):
        def one(p, _):
            slot = 0
            for j in range(2 * CTX):
                slot = jnp.maximum(slot, jnp.where(order[j] == p, j, 0))
            inverse[p] = slot
            inverse[2 * CTX - 1 - p] = slot + 1 - 2 * (slot % 2)
            return 0

        lax.fori_loop(first, first + count, one, 0)

    stage_keys(1, types_b, kb, vb)
    greeted()
    kvb_copies = exchange(0, stage_kv.at[1], in_kvb, z * GROUP + m)
    in_kvb[z * GROUP + m] = stage_kv[1, m]
    spread_b(1, 0)
    stage_rows(1, qb)
    qb_copies = exchange(1, stage_q.at[1], in_qb, m)
    kvb_copies[0].wait_recv()
    spread_b(1, 1)
    in_qb[m] = stage_q[1, m]
    stage_rows(2, go)
    go_copies = exchange(2, stage_q.at[2], in_go, m)
    in_go[m] = stage_q[2, m]
    for d in (1, 2):
        kvb_copies[d].wait_recv()
        spread_b(1, d + 1)
    stage_keys(0, types_f, kf, vf)
    spread_b(2, 0)
    kvf_copies = exchange(3, stage_kv.at[0], in_kvf, z * GROUP + m)
    in_kvf[z * GROUP + m] = stage_kv[0, m]
    spread_b(2, 1)
    stage_rows(0, qf)
    qf_copies = exchange(4, stage_q.at[0], in_qf, m)
    in_qf[m] = stage_q[0, m]
    spread_b(2, 2)
    stage_rows(3, gate)
    gate_copies = exchange(6, stage_q.at[3], in_gate, m)
    in_gate[m] = stage_q[3, m]
    spread_b(2, 3)
    for d in range(GROUP):
        invert(d * CTX // GROUP, CTX // GROUP)
        spread_b(3, d)
    for d in range(GROUP):
        spread_b(4, d)
    arrive(kvf_copies)
    for part in range(2):
        spread_f(1, part)
    gathered(1)
    arrive(qb_copies)
    arrive(go_copies)


    first = [order[2 * GROUP * z + 2 * i] for i in range(GROUP)]
    second = [order[2 * GROUP * z + 2 * i + 1] for i in range(GROUP)]
    low = [jnp.minimum(a, b) for a, b in zip(first, second)]
    low_half = [jnp.where(a < b, 0, 1) for a, b in zip(first, second)]
    quart = [a * HALF // BLOCK for a in low]
    last = TOKENS // BLOCK - 1
    stretch = [low, [2 * CTX - 1 - a for a in low]]
    span = [slice(i * QROWS, (i + 1) * QROWS) for i in range(GROUP)]
    row_in = lax.broadcasted_iota(jnp.int32, (QROWS, HEAD), 0) % HALF

    def shrink_rows(position):
        return lax.rsqrt((position * HALF + row_in + 1).astype(F32))

    def query_rows(source, i, w):
        half = low_half[i] if w == 0 else 1 - low_half[i]
        return source[i, half].reshape(QROWS, HEAD)

    def choice(i, n):
        is_low = n <= quart[i]
        return is_low, jnp.where(is_low, n, last - n), jnp.where(is_low, 0, 1)

    def bound_low(i, n):
        return jnp.where(n == quart[i], low[i] * HALF - n * BLOCK, BLOCK)

    def bound_high(i):
        return stretch[1][i] * HALF - (last - quart[i]) * BLOCK

    def put_rows(target, i, low_rows, high_rows):
        shape = (4, HALF, HEAD)
        a, b = low_rows.astype(BF).reshape(shape), high_rows.astype(BF).reshape(shape)
        target[i, 0] = jnp.where(low_half[i] == 0, a, b)
        target[i, 1] = jnp.where(low_half[i] == 0, b, a)

    def unsort(source):
        def fill(b, _):
            for k in range(BLOCK // HALF):
                j = inverse[b * (BLOCK // HALF) + k]
                ks[b, k * HALF : (k + 1) * HALF] = source[j // 2, 0, j % 2]
                vs[b, k * HALF : (k + 1) * HALF] = source[j // 2, 1, j % 2]
            return 0

        lax.fori_loop(0, last + 1, fill, 0)


    unsort(in_kvb)

    def turn(b, _):
        kt[b] = ks[b].T
        return 0

    lax.fori_loop(0, last + 1, turn, 0)
    for i in range(GROUP):
        for w in range(2):
            qs[w, i] = query_rows(in_qb, i, w)
            g = query_rows(in_go, i, w).astype(F32) * shrink_rows(stretch[w][i])
            gs[w, i] = g.astype(BF)
    key_over = lax.broadcasted_iota(jnp.int32, (BLOCK, QROWS), 0) - (
        lax.broadcasted_iota(jnp.int32, (BLOCK, QROWS), 1) % HALF
    )

    def slopes(k, v, q, g):
        u = dot_nt(k, q) * (0.5 * SCALE)
        grad = dot_nt(v, g)
        t = jnp.tanh(u)
        ut = u * t
        return u + ut, (0.5 + 0.5 * t) * (1.0 + (u - ut)) * grad

    def seen(over, bound, value):
        return jnp.where(over <= bound, value, 0.0).astype(BF)

    def backward_full(b, _):
        q, g = qs[1].reshape(GROUP * QROWS, HEAD), gs[1].reshape(GROUP * QROWS, HEAD)
        p, s = slopes(ks[b], vs[b], q, g)
        p = p.astype(BF)
        s = s.astype(BF)
        dv[stretches(b)] = dot_nn(p, g).reshape(-1, HALF, HEAD)
        dk[stretches(b)] = dot_nn(s, q).reshape(-1, HALF, HEAD)
        acc_t[1] += dot_nn(kt[b], s)
        return 0

    def backward_edge(i):
        at = last - quart[i]
        q, g = qs[1, i], gs[1, i]
        p, s = slopes(ks[at], vs[at], q, g)
        p = seen(key_over, bound_high(i), p)
        s = seen(key_over, bound_high(i), s)
        dgv[i] = dot_nn(p, g)
        dgk[i] = dot_nn(s, q)
        acc_t[1, :, span[i]] += dot_nn(kt[at], s)

    def backward_choice(n, _):
        zero = jnp.zeros((QROWS, HEAD), BF)
        ps, ss = [], []
        for i in range(GROUP):
            is_low, at, w = choice(i, n)
            q, g = qs[w, i], gs[w, i]
            p, s = slopes(ks[at], vs[at], q, g)
            p = seen(key_over, bound_low(i, n), p)
            s = seen(key_over, bound_low(i, n), s)
            part = dot_nn(kt[at], s)
            acc_t[0, :, span[i]] += jnp.where(is_low, part, 0.0)
            acc_t[1, :, span[i]] += jnp.where(is_low, 0.0, part)
            g_pick[span[i], :HEAD] = jnp.where(is_low, g, zero)
            g_pick[span[i], HEAD:] = jnp.where(is_low, zero, g)
            q_pick[span[i], :HEAD] = jnp.where(is_low, q, zero)
            q_pick[span[i], HEAD:] = jnp.where(is_low, zero, q)
            ps.append(p)
            ss.append(s)
        both_v = dot_nn(jnp.concatenate(ps, 1), g_pick[...])
        both_k = dot_nn(jnp.concatenate(ss, 1), q_pick[...])
        dv[stretches(n)] += both_v[:, :HEAD].reshape(-1, HALF, HEAD)
        dk[stretches(n)] += both_k[:, :HEAD].reshape(-1, HALF, HEAD)
        high_v, high_k = both_v[:, HEAD:], both_k[:, HEAD:]
        for i in range(GROUP):
            here = jnp.where(n == quart[i], 1.0, 0.0)
            high_v += dgv[i] * here
            high_k += dgk[i] * here
        dv[stretches(last - n)] = high_v.reshape(-1, HALF, HEAD)
        dk[stretches(last - n)] = high_k.reshape(-1, HALF, HEAD)
        return 0

    half_blocks = (last + 1) // 2
    middle = half_blocks // 2
    acc_t[...] = jnp.zeros_like(acc_t)
    spread_f(2, 0)
    lax.fori_loop(0, 3, backward_full, 0)
    spread_f(2, 1)
    lax.fori_loop(3, 6, backward_full, 0)
    spread_f(3, 0)
    lax.fori_loop(6, half_blocks, backward_full, 0)
    for i in range(GROUP):
        backward_edge(i)
    spread_f(3, 1)
    lax.fori_loop(0, 2, backward_choice, 0)
    for part in range(2):
        spread_f(4, part)
    lax.fori_loop(2, half_blocks, backward_choice, 0)


    def store_chunk(distance):
        chunk = ((z + distance + RING) % RING) * GROUP

        def store(c, _):
            for half in range(2):
                p = order[2 * (chunk + c) + half]
                dkv[chunk + c, 0, half] = (dk[p] * SCALE).astype(BF)
                dkv[chunk + c, 1, half] = dv[p].astype(BF)
            return 0

        lax.fori_loop(0, GROUP, store, 0)

    reducing = {}

    def reduce(step, lane, part):
        way = (1, -1)[lane]
        chunk = ((z + way * (RING // 2 - step) + RING) % RING) * GROUP
        mine = pl.ds(chunk + chips[part], 2)
        if step == 0 or (step == 1 and part != lane):
            source = dkv.at[mine]
        else:
            reducing[lane, part].wait_recv()
            arrived = landed[lane, step - 1, part].astype(F32)
            sums[lane, step - 1, part] = (dkv[mine].astype(F32) + arrived).astype(BF)
            source = sums.at[lane, step - 1, part]
        copy = remote(
            source, landed.at[lane, step, part],
            r_send.at[lane, step, part], r_recv.at[lane, step, part], ctx_of(z + way, m),
        )
        copy.start()
        started.append(copy)
        reducing[lane, part] = copy

    def reduce_fresh(step):
        for lane in range(2):
            reduce(step, lane, 1 - lane)

    def reduce_chained(step):
        for lane in range(2):
            reduce(step, lane, lane)

    store_chunk(RING // 2)
    reduce_chained(0)
    for distance in (3, -3):
        store_chunk(distance)
    reduce_fresh(1)
    for i in range(GROUP):
        put_rows(
            dq, i, (acc_t[0, :, span[i]] * SCALE).T, (acc_t[1, :, span[i]] * SCALE).T
        )
    dq_copies = exchange(5, dq, dq_in, m)
    dq_in[m] = dq[m]
    for distance in (2, -2, 1, -1, 0):
        store_chunk(distance)


    gathered(0)
    arrive(qf_copies)
    unsort(in_kvf)
    for i in range(GROUP):
        for w in range(2):
            qs[w, i] = query_rows(in_qf, i, w)
    query_over = lax.broadcasted_iota(jnp.int32, (QROWS, BLOCK), 1) - (
        lax.broadcasted_iota(jnp.int32, (QROWS, BLOCK), 0) % HALF
    )

    def weigh(q, k):
        u = dot_nt(q, k) * (0.5 * SCALE)
        return u + u * jnp.tanh(u)

    def forward_full(part):
        pairs = slice(2 * part, 2 * part + 2)
        rows = slice(2 * part * QROWS, 2 * (part + 1) * QROWS)

        def step(b, _):
            q = qs[1, pairs].reshape(2 * QROWS, HEAD)
            acc[1, rows] += dot_nn(weigh(q, ks[b]).astype(BF), vs[b])
            return 0

        lax.fori_loop(0, half_blocks, step, 0)

    def forward_edge(part):
        for i in (2 * part, 2 * part + 1):
            at = last - quart[i]
            p = seen(query_over, bound_high(i), weigh(qs[1, i], ks[at]))
            acc[1, span[i]] += dot_nn(p, vs[at])

    def forward_choice(part, first, end):
        def step(n, _):
            for i in (2 * part, 2 * part + 1):
                is_low, at, w = choice(i, n)
                p = seen(query_over, bound_low(i, n), weigh(qs[w, i], ks[at]))
                out = dot_nn(p, vs[at])
                acc[0, span[i]] += jnp.where(is_low, out, 0.0)
                acc[1, span[i]] += jnp.where(is_low, 0.0, out)
            return 0

        lax.fori_loop(first, end, step, 0)


    norm_copies = [[], []]

    def measure_rows(part):
        for i in (2 * part, 2 * part + 1):
            shape = (4, HALF, HEAD)
            low_rows = (acc[0, span[i]] * shrink_rows(stretch[0][i])).reshape(shape)
            high_rows = (acc[1, span[i]] * shrink_rows(stretch[1][i])).reshape(shape)
            att[i, 0] = jnp.where(low_half[i] == 0, low_rows, high_rows)
            att[i, 1] = jnp.where(low_half[i] == 0, high_rows, low_rows)
            rows = att[i]
            square = jnp.sum(rows * rows, axis=1).reshape(ROWS, HEAD)
            square = jnp.sum(square, axis=1, keepdims=True)
            norms[i] = jnp.broadcast_to(square, (ROWS, HEAD)).T[:8]
        pairs = pl.ds(2 * part, 2)
        for d, p in enumerate(peers):
            copy = remote(
                norms.at[pairs], norms_in.at[d, pairs],
                n_send.at[d, part], n_recv.at[d, part], ctx_of(z, p),
            )
            copy.start()
            started.append(copy)
            norm_copies[part].append(copy)

    def hand_rows(part):
        arrive(norm_copies[part])
        for i in (2 * part, 2 * part + 1):
            row = norms[i] + norms_in[0, i] + norms_in[1, i] + norms_in[2, i]
            square = jnp.broadcast_to(row[:1], (HEAD, ROWS)).T
            factor = lax.rsqrt(square * (1.0 / (16 * HEAD)) + EPS).reshape(2, 1, HALF, HEAD)
            for g in range(4):
                cols = pl.ds(pl.multiple_of((m * 4 + g) * HEAD, HEAD), HEAD)
                gated[i, :, g] = (
                    att[i, :, g] * factor[:, 0]
                    * gain[:, cols].reshape(1, 1, HEAD)
                    * in_gate[i, :, g].astype(F32)
                ).astype(BF)
            copy = remote(
                gated.at[i], hand_in.at[m], h_send.at[i], h_recv.at[m], beside(1, i)
            )
            copy.start()
            started.append(copy)

    acc[...] = jnp.zeros_like(acc)
    forward_full(0)
    reduce_chained(1)
    forward_edge(0)
    forward_choice(0, 0, middle)
    reduce_fresh(2)
    forward_choice(0, middle, half_blocks)
    measure_rows(0)
    reduce_chained(2)
    forward_full(1)
    reduce_fresh(3)
    arrive(gate_copies)
    hand_rows(0)
    forward_edge(1)
    forward_choice(1, 0, middle)
    reduce_chained(3)
    forward_choice(1, middle, half_blocks)
    measure_rows(1)
    arrive(dq_copies)
    for h in range(GROUP):
        for g in range(4):
            for half in range(2):
                rows = slice(half * HALF, (half + 1) * HALF)
                query_grad[rows, columns(h * 4 + g)] = dq_in[h, half, g]
    hand_rows(1)


    for part in (1, 0):
        for lane in range(2):
            reducing[lane, part].wait_recv()
        total[pl.ds(chips[part], 2)] = (
            dkv[pl.ds(z * GROUP + chips[part], 2)].astype(F32)
            + landed[0, RING // 2 - 1, part].astype(F32)
            + landed[1, RING // 2 - 1, part].astype(F32)
        ).astype(BF)
        for d in ((1, 2), (0,))[1 - part]:
            copy = remote(
                total.at[peers[d]], dkv_in.at[m], a_send.at[d, 7], a_recv.at[d, 7],
                ctx_of(z, peers[d]),
            )
            copy.start()
            started.append(copy)
            moving[2, 0, d] = copy
    dkv_in[m] = total[m]
    gathered(2)
    for h in range(GROUP):
        for half in range(2):
            rows = slice(half * HALF, (half + 1) * HALF)
            key_grad[rows, columns(h)] = dkv_in[h, 0, half]
            value_grad[rows, columns(h)] = dkv_in[h, 1, half]
    for h in range(GROUP):
        remote(gated.at[h], hand_in.at[h], h_send.at[h], h_recv.at[h], beside(1, h)).wait_recv()
        for g in range(4):
            for half in range(2):
                rows = slice(half * HALF, (half + 1) * HALF)
                handed[rows, columns(h * 4 + g)] = hand_in[h, half, g]
    for copy in started:
        copy.wait_send()


def body(
    query_fwd, key_fwd, value_fwd, gate_fwd, types_fwd,
    query_bwd, key_bwd, value_bwd, grad_out, types_bwd,
    type_key, norm_gain, stretch_order,
):
    order = stretch_order[0]
    dma = pltpu.SemaphoreType.DMA
    wide, narrow = (ROWS, 16 * HEAD), (ROWS, GROUP * HEAD)
    smem = pl.BlockSpec(memory_space=pltpu.SMEM)
    part = (HALF, HEAD)
    blocks = TOKENS // BLOCK
    heads, pairs = (GROUP, 2, 4, *part), (CTX, 2, 2, *part)
    handed, query_grad, key_grad, value_grad = pl.pallas_call(
        kernel,
        out_shape=(
            jax.ShapeDtypeStruct(wide, BF),
            jax.ShapeDtypeStruct(wide, BF),
            jax.ShapeDtypeStruct(narrow, BF),
            jax.ShapeDtypeStruct(narrow, BF),
        ),
        in_specs=[smem] + [VMEM] * 12,
        out_specs=(VMEM,) * 4,
        scratch_shapes=[
            pltpu.SMEM((2 * CTX,), jnp.int32),
            pltpu.VMEM((4, *heads), BF),
            pltpu.VMEM((2, GROUP, 2, 2, *part), BF),
            pltpu.VMEM(heads, BF),
            pltpu.VMEM(heads, BF),
            pltpu.VMEM(heads, BF),
            pltpu.VMEM(heads, BF),
            pltpu.VMEM(pairs, BF),
            pltpu.VMEM(pairs, BF),
            pltpu.VMEM((blocks, BLOCK, HEAD), BF),
            pltpu.VMEM((blocks, BLOCK, HEAD), BF),
            pltpu.VMEM((blocks, HEAD, BLOCK), BF),
            pltpu.VMEM((2 * CTX, *part), F32),
            pltpu.VMEM((2 * CTX, *part), F32),
            pltpu.VMEM((2, GROUP * QROWS, HEAD), F32),
            pltpu.VMEM((2, HEAD, GROUP * QROWS), F32),
            pltpu.VMEM((2, GROUP, QROWS, HEAD), BF),
            pltpu.VMEM((2, GROUP, QROWS, HEAD), BF),
            pltpu.VMEM((GROUP, BLOCK, HEAD), F32),
            pltpu.VMEM((GROUP, BLOCK, HEAD), F32),
            pltpu.VMEM((GROUP * QROWS, 2 * HEAD), BF),
            pltpu.VMEM((GROUP * QROWS, 2 * HEAD), BF),
            pltpu.VMEM(pairs, BF),
            pltpu.VMEM((2, RING // 2 - 1, 2, 2, 2, 2, *part), BF),
            pltpu.VMEM((2, RING // 2, 2, 2, 2, 2, *part), BF),
            pltpu.VMEM((GROUP, 2, 2, *part), BF),
            pltpu.VMEM((GROUP, 2, 2, *part), BF),
            pltpu.VMEM(heads, F32),
            pltpu.VMEM((GROUP, 8, ROWS), F32),
            pltpu.VMEM((3, GROUP, 8, ROWS), F32),
            pltpu.VMEM(heads, BF),
            pltpu.VMEM(heads, BF),
            pltpu.VMEM(heads, BF),
            pltpu.VMEM(heads, BF),
            dma((3, 8)),
            dma((3, 8)),
            dma((2, RING // 2, GROUP)),
            dma((2, RING // 2, GROUP)),
            dma((2, RING // 2, 2)),
            dma((2, RING // 2, 2)),
            dma((2, RING // 2, 2)),
            dma((2, RING // 2, 2)),
            dma((3, 2)),
            dma((3, 2)),
            dma((GROUP,)),
            dma((GROUP,)),
        ],
        compiler_params=pltpu.CompilerParams(
            collective_id=0, has_side_effects=True, vmem_limit_bytes=56 * 1024 * 1024
        ),
        name="attention",
    )(
        order, types_fwd, types_bwd, type_key[0],
        query_fwd[0], key_fwd[0], value_fwd[0],
        query_bwd[0], key_bwd[0], value_bwd[0], grad_out[0], gate_fwd[0], norm_gain,
    )
    return handed[None], query_grad[None], key_grad[None], value_grad[None]


def solution(mesh):
    rows = P("pipe", "ctx", None)
    section = P("pipe", None)
    types = P("pipe", "ctx")
    return jax.shard_map(
        body,
        mesh=mesh,
        in_specs=(
            rows, rows, rows, rows, types, rows, rows, rows, rows, types,
            P("pipe", None, None), section, section,
        ),
        out_specs=(rows, rows, rows, rows),
        check_vma=False,
    )
```

```python
import jax
import jax.numpy as jnp
from jax import lax
from jax.experimental import pallas as pl
from jax.experimental.pallas import tpu as pltpu
from jax.sharding import PartitionSpec as P

HEAD = 128
ROWS = 128
HALF = 64
GROUP = 4
RING = 8
CTX = GROUP * RING
TOKENS = CTX * ROWS
QROWS = 4 * HALF
BLOCK = 256
EPS = 1e-06
SCALE = HEAD**-0.5
BF = jnp.bfloat16
F32 = jnp.float32
MESH = pl.DeviceIdType.MESH
VMEM = pl.BlockSpec(memory_space=pltpu.VMEM)


def place():
    me = lax.axis_index("ctx")
    z = me // GROUP
    m = me % GROUP
    x, c = m // 2, m % 2
    peers = (2 * x + (1 - c), 2 * (1 - x) + c, 2 * (1 - x) + (1 - c))
    return z, m, peers


def ctx_of(z, m):
    return {"ctx": ((z + RING) % RING) * GROUP + m}


def remote(src, dst, send, recv, target):
    return pltpu.make_async_remote_copy(
        src_ref=src,
        dst_ref=dst,
        send_sem=send,
        recv_sem=recv,
        device_id=target,
        device_id_type=MESH,
    )


def greet(targets):
    barrier = pltpu.get_barrier_semaphore()
    for target in targets:
        pl.semaphore_signal(barrier, inc=1, device_id=target, device_id_type=MESH)
    return lambda: pl.semaphore_wait(barrier, len(targets))


def dot_nt(a, b):
    return lax.dot_general(a, b, (((1,), (1,)), ((), ())), preferred_element_type=F32)


def dot_nn(a, b):
    return jnp.dot(a, b, preferred_element_type=F32)


def stretches(b):
    return pl.ds(b * (BLOCK // HALF), BLOCK // HALF)


def columns(i):
    return slice(i * HEAD, (i + 1) * HEAD)


def kernel(
    order, types_f, types_b, table, qf, kf, vf, qb, kb, vb, go, gate, gain,
    handed, query_grad, key_grad, value_grad,
    inverse, stage_q, stage_kv, in_qf, in_qb, in_go, in_gate, in_kvf, in_kvb,
    ks, vs, kt, dk, dv, acc, acc_t, qs, gs, qt, gt, dgk, dgv, q_wide, g_wide,
    dkv, sums, landed, landed_half, total, dkv_in, att, norms, norms_in, dq, dq_in, gated, hand_in,
    a_send, a_recv, b_send, b_recv, g_send, g_recv, r_send, r_recv,
    n_send, n_recv, h_send, h_recv,
):
    z, m, peers = place()
    x = m // 2
    members = (m, *peers)
    chips = (2 * x, 2 * (1 - x))
    sections = lax.axis_size("pipe")
    section = lax.axis_index("pipe")

    def beside(distance, member):
        return {
            "pipe": (section + distance + sections) % sections,
            "ctx": z * GROUP + member,
        }

    greeted = greet(
        [ctx_of(z, p) for p in peers]
        + [ctx_of(z + 1, m), ctx_of(z - 1, m)]
        + [beside(d, s) for d in (1, -1) for s in range(GROUP)]
    )
    sent = []


    def exchange(t, source, target, slot):
        copies = []
        for d, p in enumerate(peers):
            copy = remote(
                source.at[p], target.at[slot], a_send.at[t], a_recv.at[d, t], ctx_of(z, p)
            )
            copy.start()
            copies.append(copy)
        sent.append((source.at[pl.ds(0, len(peers))], a_send.at[t]))
        return copies

    def stage_keys(t, types, keys, values):
        kinds = lax.broadcasted_iota(jnp.int32, (table.shape[0], ROWS), 0)
        onehot = jnp.where(kinds == types[...], 1.0, 0.0).astype(BF)
        rows = lax.dot_general(
            onehot, table[...], (((0,), (0,)), ((), ())), preferred_element_type=F32
        )
        typed = (keys[...].astype(F32) + rows).astype(BF)
        for h in range(GROUP):
            for half in range(2):
                rows = slice(half * HALF, (half + 1) * HALF)
                stage_kv[t, h, 0, half] = typed[rows, columns(h)]
                stage_kv[t, h, 1, half] = values[rows, columns(h)]

    def stage_rows(t, source):
        for h in range(GROUP):
            for g in range(4):
                for half in range(2):
                    rows = slice(half * HALF, (half + 1) * HALF)
                    stage_q[t, h, half, g] = source[rows, columns(h * 4 + g)]

    def arrive(copies):
        for copy in copies:
            copy.wait_recv()


    moving = {}

    def ring_hop(t, target, first, count, step, lane, part, send, recv):
        way = (1, -1)[lane]
        if step > 1:
            moving[t, lane, part].wait_recv()
        chunk = ((z - way * (step - 1) + RING) % RING) * GROUP
        view = target.at[pl.ds(chunk + first, count)]
        copy = remote(
            view, view, send.at[lane], recv.at[lane, step - 1, part], ctx_of(z + way, m)
        )
        copy.start()
        moving[t, lane, part] = copy

    def spread_b(step, d):
        for lane in range(2):
            if step < RING // 2 or d % 2 == lane:
                ring_hop(1, in_kvb, members[d], 1, step, lane, d, b_send, b_recv)

    def spread_f(step, part):
        for lane in range(2):
            if step < RING // 2 or part == lane:
                ring_hop(0, in_kvf, chips[part], 2, step, lane, part, g_send, g_recv)

    def gathered(t):
        for (kind, _, _), copy in moving.items():
            if kind == t:
                copy.wait_recv()

    def invert(first, count):
        def one(p, _):
            slot = 0
            for j in range(2 * CTX):
                slot = jnp.maximum(slot, jnp.where(order[j] == p, j, 0))
            inverse[p] = slot
            inverse[2 * CTX - 1 - p] = slot + 1 - 2 * (slot % 2)
            return 0

        lax.fori_loop(first, first + count, one, 0)

    stage_keys(1, types_b, kb, vb)
    greeted()
    kvb_copies = exchange(0, stage_kv.at[1], in_kvb, z * GROUP + m)
    in_kvb[z * GROUP + m] = stage_kv[1, m]
    spread_b(1, 0)
    stage_rows(1, qb)
    qb_copies = exchange(1, stage_q.at[1], in_qb, m)
    kvb_copies[0].wait_recv()
    spread_b(1, 1)
    in_qb[m] = stage_q[1, m]
    stage_rows(2, go)
    go_copies = exchange(2, stage_q.at[2], in_go, m)
    in_go[m] = stage_q[2, m]
    for d in (1, 2):
        kvb_copies[d].wait_recv()
        spread_b(1, d + 1)
    stage_keys(0, types_f, kf, vf)
    spread_b(2, 0)
    kvf_copies = exchange(3, stage_kv.at[0], in_kvf, z * GROUP + m)
    in_kvf[z * GROUP + m] = stage_kv[0, m]
    spread_b(2, 1)
    stage_rows(0, qf)
    qf_copies = exchange(4, stage_q.at[0], in_qf, m)
    in_qf[m] = stage_q[0, m]
    spread_b(2, 2)
    stage_rows(3, gate)
    gate_copies = exchange(6, stage_q.at[3], in_gate, m)
    in_gate[m] = stage_q[3, m]
    spread_b(2, 3)
    for d in range(GROUP):
        invert(d * CTX // GROUP, CTX // GROUP)
        spread_b(3, d)
    for d in range(GROUP):
        spread_b(4, d)
    arrive(kvf_copies)
    for part in range(2):
        spread_f(1, part)
    gathered(1)
    arrive(qb_copies)
    arrive(go_copies)


    first = [order[2 * GROUP * z + 2 * i] for i in range(GROUP)]
    second = [order[2 * GROUP * z + 2 * i + 1] for i in range(GROUP)]
    low = [jnp.minimum(a, b) for a, b in zip(first, second)]
    low_half = [jnp.where(a < b, 0, 1) for a, b in zip(first, second)]
    quart = [a * HALF // BLOCK for a in low]
    last = TOKENS // BLOCK - 1
    stretch = [low, [2 * CTX - 1 - a for a in low]]
    span = [slice(i * QROWS, (i + 1) * QROWS) for i in range(GROUP)]
    row_in = lax.broadcasted_iota(jnp.int32, (QROWS, HEAD), 0) % HALF

    def shrink_rows(position):
        return lax.rsqrt((position * HALF + row_in + 1).astype(F32))

    def query_rows(source, i, w):
        half = low_half[i] if w == 0 else 1 - low_half[i]
        return source[i, half].reshape(QROWS, HEAD)

    def choice(i, n):
        is_low = n <= quart[i]
        return is_low, jnp.where(is_low, n, last - n), jnp.where(is_low, 0, 1)

    def bound_low(i, n):
        return jnp.where(n == quart[i], low[i] * HALF - n * BLOCK, BLOCK)

    def bound_high(i):
        return stretch[1][i] * HALF - (last - quart[i]) * BLOCK

    def put_rows(target, i, low_rows, high_rows):
        shape = (4, HALF, HEAD)
        a, b = low_rows.astype(BF).reshape(shape), high_rows.astype(BF).reshape(shape)
        target[i, 0] = jnp.where(low_half[i] == 0, a, b)
        target[i, 1] = jnp.where(low_half[i] == 0, b, a)

    def unsort(source):
        def fill(b, _):
            for k in range(BLOCK // HALF):
                j = inverse[b * (BLOCK // HALF) + k]
                ks[b, k * HALF : (k + 1) * HALF] = source[j // 2, 0, j % 2]
                vs[b, k * HALF : (k + 1) * HALF] = source[j // 2, 1, j % 2]
            return 0

        lax.fori_loop(0, last + 1, fill, 0)


    unsort(in_kvb)

    def turn(b, _):
        kt[b] = ks[b].T
        return 0

    lax.fori_loop(0, last + 1, turn, 0)
    for i in range(GROUP):
        for w in range(2):
            qs[w, i] = query_rows(in_qb, i, w)
            g = query_rows(in_go, i, w).astype(F32) * (0.5 * shrink_rows(stretch[w][i]))
            gs[w, i] = g.astype(BF)
            qt[w, :, span[i]] = qs[w, i].T
            gt[w, :, span[i]] = gs[w, i].T
            q_wide[w, i] = jnp.zeros((QROWS, 2 * HEAD), BF)
            q_wide[w, i, :, columns(w)] = qs[w, i]
            g_wide[w, i] = jnp.zeros((QROWS, 2 * HEAD), BF)
            g_wide[w, i, :, columns(w)] = gs[w, i]
    key_over = lax.broadcasted_iota(jnp.int32, (BLOCK, QROWS), 0) - (
        lax.broadcasted_iota(jnp.int32, (BLOCK, QROWS), 1) % HALF
    )

    def slopes(k, v, q, g):
        u = (dot_nn(k, q) * (0.5 * SCALE)).astype(BF)
        grad = dot_nn(v, g).astype(BF)
        one = jnp.asarray(1.0, BF)
        t = jnp.tanh(u)
        ut = u * t
        return u + ut, (one + t) * (one + (u - ut)) * grad

    def seen(over, bound, value):
        return jnp.where(over <= bound, value, jnp.zeros_like(value)).astype(BF)

    def backward_full(b, _):
        q, g = qs[1].reshape(GROUP * QROWS, HEAD), gs[1].reshape(GROUP * QROWS, HEAD)
        p, s = slopes(ks[b], vs[b], qt[1], gt[1])
        dv[stretches(b)] = dot_nn(p, g).reshape(-1, HALF, HEAD)
        dk[stretches(b)] = dot_nn(s, q).reshape(-1, HALF, HEAD)
        acc_t[1] += dot_nn(kt[b], s)
        return 0

    def backward_edge(i):
        at = last - quart[i]
        p, s = slopes(ks[at], vs[at], qt[1, :, span[i]], gt[1, :, span[i]])
        p = seen(key_over, bound_high(i), p)
        s = seen(key_over, bound_high(i), s)
        dgv[i] = dot_nn(p, gs[1, i])
        dgk[i] = dot_nn(s, qs[1, i])
        acc_t[1, :, span[i]] += dot_nn(kt[at], s)

    def backward_choice(n, _):
        ps, ss, qw, gw = [], [], [], []
        for i in range(GROUP):
            is_low, at, w = choice(i, n)
            p, s = slopes(ks[at], vs[at], qt[w, :, span[i]], gt[w, :, span[i]])
            p = seen(key_over, bound_low(i, n), p)
            s = seen(key_over, bound_low(i, n), s)
            part = dot_nn(kt[at], s)
            acc_t[0, :, span[i]] += jnp.where(is_low, part, 0.0)
            acc_t[1, :, span[i]] += jnp.where(is_low, 0.0, part)
            ps.append(p)
            ss.append(s)
            qw.append(q_wide[w, i])
            gw.append(g_wide[w, i])
        both_v = dot_nn(jnp.concatenate(ps, 1), jnp.concatenate(gw, 0))
        both_k = dot_nn(jnp.concatenate(ss, 1), jnp.concatenate(qw, 0))
        dv[stretches(n)] += both_v[:, :HEAD].reshape(-1, HALF, HEAD)
        dk[stretches(n)] += both_k[:, :HEAD].reshape(-1, HALF, HEAD)
        high_v, high_k = both_v[:, HEAD:], both_k[:, HEAD:]
        for i in range(GROUP):
            here = jnp.where(n == quart[i], 1.0, 0.0)
            high_v += dgv[i] * here
            high_k += dgk[i] * here
        dv[stretches(last - n)] = high_v.reshape(-1, HALF, HEAD)
        dk[stretches(last - n)] = high_k.reshape(-1, HALF, HEAD)
        return 0

    half_blocks = (last + 1) // 2
    middle = half_blocks // 2
    acc_t[...] = jnp.zeros_like(acc_t)
    spread_f(2, 0)
    lax.fori_loop(0, 3, backward_full, 0)
    spread_f(2, 1)
    lax.fori_loop(3, 6, backward_full, 0)
    spread_f(3, 0)
    lax.fori_loop(6, half_blocks, backward_full, 0)
    for i in range(GROUP):
        backward_edge(i)
    spread_f(3, 1)
    lax.fori_loop(0, 2, backward_choice, 0)
    for part in range(2):
        spread_f(4, part)
    lax.fori_loop(2, half_blocks, backward_choice, 0)


    def store_chunk(distance):
        chunk = ((z + distance + RING) % RING) * GROUP

        def store(c, _):
            for half in range(2):
                p = order[2 * (chunk + c) + half]
                dkv[chunk + c, 0, half] = (dk[p] * SCALE).astype(BF)
                dkv[chunk + c, 1, half] = (dv[p] * 2.0).astype(BF)
            return 0

        lax.fori_loop(0, GROUP, store, 0)

    reducing = {}

    def reduce(step, part):
        for lane, way in enumerate((1, -1)):
            chunk = ((z + way * (RING // 2 - step) + RING) % RING) * GROUP
            mine = pl.ds(chunk + chips[part], 2)
            if step > 0:
                reducing[lane, part].wait_recv()
                terms = dkv[mine].astype(F32)
                partial = sums.at[lane, step - 1, part]
            if step == 0:
                source, target = dkv.at[mine, :, lane], landed_half.at[lane, part]
            else:
                if step == 1:
                    arrived = landed_half[lane, part].astype(F32)
                    partial[:, :, lane] = (terms[:, :, lane] + arrived).astype(BF)
                    partial[:, :, 1 - lane] = dkv[mine, :, 1 - lane]
                else:
                    arrived = landed[lane, step - 2, part].astype(F32)
                    partial[...] = (terms + arrived).astype(BF)
                source, target = partial, landed.at[lane, step - 1, part]
            copy = remote(
                source, target, r_send.at[lane], r_recv.at[lane, step, part],
                ctx_of(z + way, m),
            )
            copy.start()
            reducing[lane, part] = copy

    store_chunk(RING // 2)
    reduce(0, 1)
    reduce(0, 0)
    for distance in (3, -3):
        store_chunk(distance)
    for i in range(GROUP):
        put_rows(
            dq, i, (acc_t[0, :, span[i]] * SCALE).T, (acc_t[1, :, span[i]] * SCALE).T
        )
    dq_copies = exchange(5, dq, dq_in, m)
    dq_in[m] = dq[m]
    for distance in (2, -2, 1, -1, 0):
        store_chunk(distance)


    gathered(0)
    arrive(qf_copies)
    unsort(in_kvf)
    for i in range(GROUP):
        for w in range(2):
            qs[w, i] = query_rows(in_qf, i, w)
    query_over = lax.broadcasted_iota(jnp.int32, (QROWS, BLOCK), 1) - (
        lax.broadcasted_iota(jnp.int32, (QROWS, BLOCK), 0) % HALF
    )

    def weigh(q, k):
        u = dot_nt(q, k) * (0.5 * SCALE)
        return u + u * jnp.tanh(u)

    def forward_full(part):
        pairs = slice(2 * part, 2 * part + 2)
        rows = slice(2 * part * QROWS, 2 * (part + 1) * QROWS)

        def step(b, _):
            q = qs[1, pairs].reshape(2 * QROWS, HEAD)
            acc[1, rows] += dot_nn(weigh(q, ks[b]).astype(BF), vs[b])
            return 0

        lax.fori_loop(0, half_blocks, step, 0)

    def forward_edge(part):
        for i in (2 * part, 2 * part + 1):
            at = last - quart[i]
            p = seen(query_over, bound_high(i), weigh(qs[1, i], ks[at]))
            acc[1, span[i]] += dot_nn(p, vs[at])

    def forward_choice(part, first, end):
        def step(n, _):
            for i in (2 * part, 2 * part + 1):
                is_low, at, w = choice(i, n)
                p = seen(query_over, bound_low(i, n), weigh(qs[w, i], ks[at]))
                out = dot_nn(p, vs[at])
                acc[0, span[i]] += jnp.where(is_low, out, 0.0)
                acc[1, span[i]] += jnp.where(is_low, 0.0, out)
            return 0

        lax.fori_loop(first, end, step, 0)


    norm_copies = [[], []]

    def measure_rows(part):
        for i in (2 * part, 2 * part + 1):
            shape = (4, HALF, HEAD)
            low_rows = (acc[0, span[i]] * shrink_rows(stretch[0][i])).reshape(shape)
            high_rows = (acc[1, span[i]] * shrink_rows(stretch[1][i])).reshape(shape)
            att[i, 0] = jnp.where(low_half[i] == 0, low_rows, high_rows)
            att[i, 1] = jnp.where(low_half[i] == 0, high_rows, low_rows)
            rows = att[i]
            square = jnp.sum(rows * rows, axis=1).reshape(ROWS, HEAD)
            square = jnp.sum(square, axis=1, keepdims=True)
            norms[i] = jnp.broadcast_to(square, (ROWS, HEAD)).T[:8]
        pairs = pl.ds(2 * part, 2)
        for d, p in enumerate(peers):
            copy = remote(
                norms.at[pairs], norms_in.at[d, pairs],
                n_send, n_recv.at[d, part], ctx_of(z, p),
            )
            copy.start()
            norm_copies[part].append(copy)

    def hand_rows(part):
        arrive(norm_copies[part])
        for i in (2 * part, 2 * part + 1):
            row = norms[i] + norms_in[0, i] + norms_in[1, i] + norms_in[2, i]
            square = jnp.broadcast_to(row[:1], (HEAD, ROWS)).T
            factor = lax.rsqrt(square * (1.0 / (16 * HEAD)) + EPS).reshape(2, 1, HALF, HEAD)
            for g in range(4):
                cols = pl.ds(pl.multiple_of((m * 4 + g) * HEAD, HEAD), HEAD)
                gated[i, :, g] = (
                    att[i, :, g] * factor[:, 0]
                    * gain[:, cols].reshape(1, 1, HEAD)
                    * in_gate[i, :, g].astype(F32)
                ).astype(BF)
            copy = remote(
                gated.at[i], hand_in.at[m], h_send, h_recv.at[m], beside(1, i)
            )
            copy.start()

    acc[...] = jnp.zeros_like(acc)
    forward_full(0)
    reduce(1, 1)
    reduce(1, 0)
    forward_edge(0)
    forward_choice(0, 0, half_blocks)
    measure_rows(0)
    reduce(2, 1)
    forward_full(1)
    reduce(2, 0)
    arrive(gate_copies)
    hand_rows(0)
    forward_edge(1)
    forward_choice(1, 0, half_blocks)
    measure_rows(1)
    reduce(3, 1)
    hand_rows(1)
    reduce(3, 0)
    arrive(dq_copies)
    for h in range(GROUP):
        for g in range(4):
            for half in range(2):
                rows = slice(half * HALF, (half + 1) * HALF)
                query_grad[rows, columns(h * 4 + g)] = dq_in[h, half, g]


    for part in (1, 0):
        for lane in range(2):
            reducing[lane, part].wait_recv()
        total[pl.ds(chips[part], 2)] = (
            dkv[pl.ds(z * GROUP + chips[part], 2)].astype(F32)
            + landed[0, RING // 2 - 2, part].astype(F32)
            + landed[1, RING // 2 - 2, part].astype(F32)
        ).astype(BF)
        for d in ((1, 2), (0,))[1 - part]:
            copy = remote(
                total.at[peers[d]], dkv_in.at[m], a_send.at[7], a_recv.at[d, 7],
                ctx_of(z, peers[d]),
            )
            copy.start()
            moving[2, 0, d] = copy
    dkv_in[m] = total[m]
    gathered(2)
    for h in range(GROUP):
        for half in range(2):
            rows = slice(half * HALF, (half + 1) * HALF)
            key_grad[rows, columns(h)] = dkv_in[h, 0, half]
            value_grad[rows, columns(h)] = dkv_in[h, 1, half]
    for h in range(GROUP):
        remote(gated.at[h], hand_in.at[h], h_send, h_recv.at[h], beside(1, h)).wait_recv()
        for g in range(4):
            for half in range(2):
                rows = slice(half * HALF, (half + 1) * HALF)
                handed[rows, columns(h * 4 + g)] = hand_in[h, half, g]
    ring = pl.ds(0, GROUP * RING // 2 - 2)
    for lane in range(2):
        sent.append((in_kvb.at[ring], b_send.at[lane]))
        sent.append((in_kvf.at[ring], g_send.at[lane]))
        sent.append((dkv.at[ring], r_send.at[lane]))
    sent.append((total.at[pl.ds(0, len(peers))], a_send.at[7]))
    sent.append((norms_in, n_send))
    sent.append((gated, h_send))
    for view, send in sent:
        remote(view, view, send, h_recv.at[0], ctx_of(z, peers[0])).wait_send()


def copy_kernel(*refs):
    for source, target in zip(refs[:4], refs[4:], strict=True):
        target[...] = source[...]


def body(
    query_fwd, key_fwd, value_fwd, gate_fwd, types_fwd,
    query_bwd, key_bwd, value_bwd, grad_out, types_bwd,
    type_key, norm_gain, stretch_order,
):
    order = stretch_order[0]
    dma = pltpu.SemaphoreType.DMA
    wide, narrow = (ROWS, 16 * HEAD), (ROWS, GROUP * HEAD)
    smem = pl.BlockSpec(memory_space=pltpu.SMEM)
    part = (HALF, HEAD)
    blocks = TOKENS // BLOCK
    heads, pairs = (GROUP, 2, 4, *part), (CTX, 2, 2, *part)
    handed, query_grad, key_grad, value_grad = pl.pallas_call(
        kernel,
        out_shape=(
            jax.ShapeDtypeStruct(wide, BF),
            jax.ShapeDtypeStruct(wide, BF),
            jax.ShapeDtypeStruct(narrow, BF),
            jax.ShapeDtypeStruct(narrow, BF),
        ),
        in_specs=[smem] + [VMEM] * 12,
        out_specs=(VMEM,) * 4,
        scratch_shapes=[
            pltpu.SMEM((2 * CTX,), jnp.int32),
            pltpu.VMEM((4, *heads), BF),
            pltpu.VMEM((2, GROUP, 2, 2, *part), BF),
            pltpu.VMEM(heads, BF),
            pltpu.VMEM(heads, BF),
            pltpu.VMEM(heads, BF),
            pltpu.VMEM(heads, BF),
            pltpu.VMEM(pairs, BF),
            pltpu.VMEM(pairs, BF),
            pltpu.VMEM((blocks, BLOCK, HEAD), BF),
            pltpu.VMEM((blocks, BLOCK, HEAD), BF),
            pltpu.VMEM((blocks, HEAD, BLOCK), BF),
            pltpu.VMEM((2 * CTX, *part), F32),
            pltpu.VMEM((2 * CTX, *part), F32),
            pltpu.VMEM((2, GROUP * QROWS, HEAD), F32),
            pltpu.VMEM((2, HEAD, GROUP * QROWS), F32),
            pltpu.VMEM((2, GROUP, QROWS, HEAD), BF),
            pltpu.VMEM((2, GROUP, QROWS, HEAD), BF),
            pltpu.VMEM((2, HEAD, GROUP * QROWS), BF),
            pltpu.VMEM((2, HEAD, GROUP * QROWS), BF),
            pltpu.VMEM((GROUP, BLOCK, HEAD), F32),
            pltpu.VMEM((GROUP, BLOCK, HEAD), F32),
            pltpu.VMEM((2, GROUP, QROWS, 2 * HEAD), BF),
            pltpu.VMEM((2, GROUP, QROWS, 2 * HEAD), BF),
            pltpu.VMEM(pairs, BF),
            pltpu.VMEM((2, RING // 2 - 1, 2, 2, 2, 2, *part), BF),
            pltpu.VMEM((2, RING // 2 - 1, 2, 2, 2, 2, *part), BF),
            pltpu.VMEM((2, 2, 2, 2, *part), BF),
            pltpu.VMEM((GROUP, 2, 2, *part), BF),
            pltpu.VMEM((GROUP, 2, 2, *part), BF),
            pltpu.VMEM(heads, F32),
            pltpu.VMEM((GROUP, 8, ROWS), F32),
            pltpu.VMEM((3, GROUP, 8, ROWS), F32),
            pltpu.VMEM(heads, BF),
            pltpu.VMEM(heads, BF),
            pltpu.VMEM(heads, BF),
            pltpu.VMEM(heads, BF),
            dma((8,)),
            dma((3, 8)),
            dma((2,)),
            dma((2, RING // 2, GROUP)),
            dma((2,)),
            dma((2, RING // 2, 2)),
            dma((2,)),
            dma((2, RING // 2, 2)),
            dma,
            dma((3, 2)),
            dma,
            dma((GROUP,)),
        ],
        compiler_params=pltpu.CompilerParams(
            collective_id=0, has_side_effects=True, vmem_limit_bytes=56 * 1024 * 1024
        ),
        name="attention",
    )(
        order, types_fwd, types_bwd, type_key[0],
        query_fwd[0], key_fwd[0], value_fwd[0],
        query_bwd[0], key_bwd[0], value_bwd[0], grad_out[0], gate_fwd[0], norm_gain,
    )
    outs = (handed, query_grad, key_grad, value_grad)
    outs = pl.pallas_call(
        copy_kernel,
        out_shape=tuple(jax.ShapeDtypeStruct(o.shape, o.dtype) for o in outs),
        in_specs=[VMEM] * 4,
        out_specs=(VMEM,) * 4,
        name="finish",
    )(*outs)
    return tuple(o[None] for o in outs)


def solution(mesh):
    rows = P("pipe", "ctx", None)
    section = P("pipe", None)
    types = P("pipe", "ctx")
    return jax.shard_map(
        body,
        mesh=mesh,
        in_specs=(
            rows, rows, rows, rows, types, rows, rows, rows, rows, types,
            P("pipe", None, None), section, section,
        ),
        out_specs=(rows, rows, rows, rows),
        check_vma=False,
    )
```

```python
import jax
import jax.numpy as jnp
from jax import lax
from jax.experimental import pallas as pl
from jax.experimental.pallas import tpu as pltpu
from jax.sharding import PartitionSpec as P

HEAD = 128
ROWS = 128
HALF = 64
GROUP = 4
RING = 8
CTX = GROUP * RING
TOKENS = CTX * ROWS
QROWS = 4 * HALF
BLOCK = 256
EPS = 1e-06
SCALE = HEAD**-0.5
BF = jnp.bfloat16
F32 = jnp.float32
MESH = pl.DeviceIdType.MESH
VMEM = pl.BlockSpec(memory_space=pltpu.VMEM)


def place():
    me = lax.axis_index("ctx")
    z = me // GROUP
    m = me % GROUP
    x, c = m // 2, m % 2
    peers = (2 * x + (1 - c), 2 * (1 - x) + c, 2 * (1 - x) + (1 - c))
    return z, m, peers


def ctx_of(z, m):
    return {"ctx": ((z + RING) % RING) * GROUP + m}


def remote(src, dst, send, recv, target):
    return pltpu.make_async_remote_copy(
        src_ref=src,
        dst_ref=dst,
        send_sem=send,
        recv_sem=recv,
        device_id=target,
        device_id_type=MESH,
    )


def greet(targets):
    barrier = pltpu.get_barrier_semaphore()
    for target in targets:
        pl.semaphore_signal(barrier, inc=1, device_id=target, device_id_type=MESH)
    return lambda: pl.semaphore_wait(barrier, len(targets))


def dot_nt(a, b):
    return lax.dot_general(a, b, (((1,), (1,)), ((), ())), preferred_element_type=F32)


def dot_nn(a, b):
    return jnp.dot(a, b, preferred_element_type=F32)


def stretches(b):
    return pl.ds(b * (BLOCK // HALF), BLOCK // HALF)


def columns(i):
    return slice(i * HEAD, (i + 1) * HEAD)


def kernel(
    order, types_f, types_b, table, kb, vb, gain, qb_far, go_far, kf_far, vf_far, qf_far, gate_far,
    handed, query_grad, key_grad, value_grad,
    inverse, stage_q, stage_kv, in_qf, in_qb, in_go, in_gate, in_kvf, in_kvb,
    ks, vs, kt, dk, dv, acc, acc_t, qs, gs, qt, gt, dgk, dgv, q_wide, g_wide,
    dkv, sums, landed, landed_half, total, dkv_in, att, norms, norms_in, dq, dq_in, gated, hand_in,
    a_send, a_recv, b_send, b_recv, g_send, g_recv, r_send, r_recv,
    n_send, n_recv, h_send, h_recv,
    qb, go, kf, vf, qf, gate, l_sem,
):
    loads = {}
    near = ((qb_far, qb), (go_far, go), (kf_far, kf), (vf_far, vf), (qf_far, qf), (gate_far, gate))
    for n, (far, here) in enumerate(near):
        loads[n] = pltpu.make_async_copy(far, here, l_sem.at[n])
        loads[n].start()
    z, m, peers = place()
    x = m // 2
    members = (m, *peers)
    chips = (2 * x, 2 * (1 - x))
    sections = lax.axis_size("pipe")
    section = lax.axis_index("pipe")

    def beside(distance, member):
        return {
            "pipe": (section + distance + sections) % sections,
            "ctx": z * GROUP + member,
        }

    greeted = greet(
        [ctx_of(z, p) for p in peers]
        + [ctx_of(z + 1, m), ctx_of(z - 1, m)]
        + [beside(d, s) for d in (1, -1) for s in range(GROUP)]
    )
    sent = []


    def exchange(t, source, target, slot):
        copies = []
        for d, p in enumerate(peers):
            copy = remote(
                source.at[p], target.at[slot], a_send.at[t], a_recv.at[d, t], ctx_of(z, p)
            )
            copy.start()
            copies.append(copy)
        sent.append((source.at[pl.ds(0, len(peers))], a_send.at[t]))
        return copies

    def stage_keys(t, types, keys, values):
        kinds = lax.broadcasted_iota(jnp.int32, (table.shape[0], ROWS), 0)
        onehot = jnp.where(kinds == types[...], 1.0, 0.0).astype(BF)
        rows = lax.dot_general(
            onehot, table[...], (((0,), (0,)), ((), ())), preferred_element_type=F32
        )
        typed = (keys[...].astype(F32) + rows).astype(BF)
        for h in range(GROUP):
            for half in range(2):
                rows = slice(half * HALF, (half + 1) * HALF)
                stage_kv[t, h, 0, half] = typed[rows, columns(h)]
                stage_kv[t, h, 1, half] = values[rows, columns(h)]

    def stage_rows(t, source):
        for h in range(GROUP):
            for g in range(4):
                for half in range(2):
                    rows = slice(half * HALF, (half + 1) * HALF)
                    stage_q[t, h, half, g] = source[rows, columns(h * 4 + g)]

    def arrive(copies):
        for copy in copies:
            copy.wait_recv()


    moving = {}

    def ring_hop(t, target, first, count, step, lane, part, send, recv):
        way = (1, -1)[lane]
        if step > 1:
            moving[t, lane, part].wait_recv()
        chunk = ((z - way * (step - 1) + RING) % RING) * GROUP
        view = target.at[pl.ds(chunk + first, count)]
        copy = remote(
            view, view, send.at[lane], recv.at[lane, step - 1, part], ctx_of(z + way, m)
        )
        copy.start()
        moving[t, lane, part] = copy

    def spread_b(step, d):
        for lane in range(2):
            if step < RING // 2 or d % 2 == lane:
                ring_hop(1, in_kvb, members[d], 1, step, lane, d, b_send, b_recv)

    def spread_f(step, part):
        for lane in range(2):
            if step < RING // 2 or part == lane:
                ring_hop(0, in_kvf, chips[part], 2, step, lane, part, g_send, g_recv)

    def gathered(t):
        for (kind, _, _), copy in moving.items():
            if kind == t:
                copy.wait_recv()

    def invert(first, count):
        def one(p, _):
            slot = 0
            for j in range(2 * CTX):
                slot = jnp.maximum(slot, jnp.where(order[j] == p, j, 0))
            inverse[p] = slot
            inverse[2 * CTX - 1 - p] = slot + 1 - 2 * (slot % 2)
            return 0

        lax.fori_loop(first, first + count, one, 0)

    stage_keys(1, types_b, kb, vb)
    greeted()
    kvb_copies = exchange(0, stage_kv.at[1], in_kvb, z * GROUP + m)
    in_kvb[z * GROUP + m] = stage_kv[1, m]
    spread_b(1, 0)
    loads[0].wait()
    stage_rows(1, qb)
    qb_copies = exchange(1, stage_q.at[1], in_qb, m)
    kvb_copies[0].wait_recv()
    spread_b(1, 1)
    in_qb[m] = stage_q[1, m]
    loads[1].wait()
    stage_rows(2, go)
    go_copies = exchange(2, stage_q.at[2], in_go, m)
    in_go[m] = stage_q[2, m]
    for d in (1, 2):
        kvb_copies[d].wait_recv()
        spread_b(1, d + 1)
    loads[2].wait()
    loads[3].wait()
    stage_keys(0, types_f, kf, vf)
    spread_b(2, 0)
    kvf_copies = exchange(3, stage_kv.at[0], in_kvf, z * GROUP + m)
    in_kvf[z * GROUP + m] = stage_kv[0, m]
    spread_b(2, 1)
    loads[4].wait()
    stage_rows(0, qf)
    qf_copies = exchange(4, stage_q.at[0], in_qf, m)
    in_qf[m] = stage_q[0, m]
    spread_b(2, 2)
    loads[5].wait()
    stage_rows(3, gate)
    gate_copies = exchange(6, stage_q.at[3], in_gate, m)
    in_gate[m] = stage_q[3, m]
    spread_b(2, 3)
    for d in range(GROUP):
        invert(d * CTX // GROUP, CTX // GROUP)
        spread_b(3, d)
    for d in range(GROUP):
        spread_b(4, d)
    arrive(kvf_copies)
    for part in range(2):
        spread_f(1, part)
    gathered(1)
    arrive(qb_copies)
    arrive(go_copies)


    first = [order[2 * GROUP * z + 2 * i] for i in range(GROUP)]
    second = [order[2 * GROUP * z + 2 * i + 1] for i in range(GROUP)]
    low = [jnp.minimum(a, b) for a, b in zip(first, second)]
    low_half = [jnp.where(a < b, 0, 1) for a, b in zip(first, second)]
    quart = [a * HALF // BLOCK for a in low]
    last = TOKENS // BLOCK - 1
    stretch = [low, [2 * CTX - 1 - a for a in low]]
    span = [slice(i * QROWS, (i + 1) * QROWS) for i in range(GROUP)]
    row_in = lax.broadcasted_iota(jnp.int32, (QROWS, HEAD), 0) % HALF

    def shrink_rows(position):
        return lax.rsqrt((position * HALF + row_in + 1).astype(F32))

    def query_rows(source, i, w):
        half = low_half[i] if w == 0 else 1 - low_half[i]
        return source[i, half].reshape(QROWS, HEAD)

    def choice(i, n):
        is_low = n <= quart[i]
        return is_low, jnp.where(is_low, n, last - n), jnp.where(is_low, 0, 1)

    def bound_low(i, n):
        return jnp.where(n == quart[i], low[i] * HALF - n * BLOCK, BLOCK)

    def bound_high(i):
        return stretch[1][i] * HALF - (last - quart[i]) * BLOCK

    def put_rows(target, i, low_rows, high_rows):
        shape = (4, HALF, HEAD)
        a, b = low_rows.astype(BF).reshape(shape), high_rows.astype(BF).reshape(shape)
        target[i, 0] = jnp.where(low_half[i] == 0, a, b)
        target[i, 1] = jnp.where(low_half[i] == 0, b, a)

    def unsort(source):
        def fill(b, _):
            for k in range(BLOCK // HALF):
                j = inverse[b * (BLOCK // HALF) + k]
                ks[b, k * HALF : (k + 1) * HALF] = source[j // 2, 0, j % 2]
                vs[b, k * HALF : (k + 1) * HALF] = source[j // 2, 1, j % 2]
            return 0

        lax.fori_loop(0, last + 1, fill, 0)


    unsort(in_kvb)

    def turn(b, _):
        kt[b] = ks[b].T
        return 0

    lax.fori_loop(0, last + 1, turn, 0)
    for i in range(GROUP):
        for w in range(2):
            qs[w, i] = query_rows(in_qb, i, w)
            g = query_rows(in_go, i, w).astype(F32) * (0.5 * shrink_rows(stretch[w][i]))
            gs[w, i] = g.astype(BF)
            qt[w, :, span[i]] = qs[w, i].T
            gt[w, :, span[i]] = gs[w, i].T
            q_wide[w, i] = jnp.zeros((QROWS, 2 * HEAD), BF)
            q_wide[w, i, :, columns(w)] = qs[w, i]
            g_wide[w, i] = jnp.zeros((QROWS, 2 * HEAD), BF)
            g_wide[w, i, :, columns(w)] = gs[w, i]
    key_over = lax.broadcasted_iota(jnp.int32, (BLOCK, QROWS), 0) - (
        lax.broadcasted_iota(jnp.int32, (BLOCK, QROWS), 1) % HALF
    )

    def slopes(k, v, q, g):
        u = (dot_nn(k, q) * (0.5 * SCALE)).astype(BF)
        grad = dot_nn(v, g).astype(BF)
        one = jnp.asarray(1.0, BF)
        t = jnp.tanh(u)
        ut = u * t
        return u + ut, (one + t) * (one + (u - ut)) * grad

    def seen(over, bound, value):
        return jnp.where(over <= bound, value, jnp.zeros_like(value)).astype(BF)

    def backward_full(b, _):
        q, g = qs[1].reshape(GROUP * QROWS, HEAD), gs[1].reshape(GROUP * QROWS, HEAD)
        p, s = slopes(ks[b], vs[b], qt[1], gt[1])
        dv[stretches(b)] = dot_nn(p, g).reshape(-1, HALF, HEAD)
        dk[stretches(b)] = dot_nn(s, q).reshape(-1, HALF, HEAD)
        acc_t[1] += dot_nn(kt[b], s)
        return 0

    def backward_edge(i):
        at = last - quart[i]
        p, s = slopes(ks[at], vs[at], qt[1, :, span[i]], gt[1, :, span[i]])
        p = seen(key_over, bound_high(i), p)
        s = seen(key_over, bound_high(i), s)
        dgv[i] = dot_nn(p, gs[1, i])
        dgk[i] = dot_nn(s, qs[1, i])
        acc_t[1, :, span[i]] += dot_nn(kt[at], s)

    def backward_choice(n, _):
        ps, ss, qw, gw = [], [], [], []
        for i in range(GROUP):
            is_low, at, w = choice(i, n)
            p, s = slopes(ks[at], vs[at], qt[w, :, span[i]], gt[w, :, span[i]])
            p = seen(key_over, bound_low(i, n), p)
            s = seen(key_over, bound_low(i, n), s)
            part = dot_nn(kt[at], s)
            acc_t[0, :, span[i]] += jnp.where(is_low, part, 0.0)
            acc_t[1, :, span[i]] += jnp.where(is_low, 0.0, part)
            ps.append(p)
            ss.append(s)
            qw.append(q_wide[w, i])
            gw.append(g_wide[w, i])
        both_v = dot_nn(jnp.concatenate(ps, 1), jnp.concatenate(gw, 0))
        both_k = dot_nn(jnp.concatenate(ss, 1), jnp.concatenate(qw, 0))
        dv[stretches(n)] += both_v[:, :HEAD].reshape(-1, HALF, HEAD)
        dk[stretches(n)] += both_k[:, :HEAD].reshape(-1, HALF, HEAD)
        high_v, high_k = both_v[:, HEAD:], both_k[:, HEAD:]
        for i in range(GROUP):
            here = jnp.where(n == quart[i], 1.0, 0.0)
            high_v += dgv[i] * here
            high_k += dgk[i] * here
        dv[stretches(last - n)] = high_v.reshape(-1, HALF, HEAD)
        dk[stretches(last - n)] = high_k.reshape(-1, HALF, HEAD)
        return 0

    half_blocks = (last + 1) // 2
    middle = half_blocks // 2
    acc_t[...] = jnp.zeros_like(acc_t)
    spread_f(2, 0)
    lax.fori_loop(0, 5, backward_full, 0)
    spread_f(2, 1)
    lax.fori_loop(5, half_blocks, backward_full, 0)
    spread_f(3, 0)
    for i in range(GROUP):
        backward_edge(i)
    lax.fori_loop(0, 2, backward_choice, 0)
    spread_f(3, 1)
    lax.fori_loop(2, 5, backward_choice, 0)
    for part in range(2):
        spread_f(4, part)
    lax.fori_loop(5, half_blocks, backward_choice, 0)


    def store_chunk(distance):
        chunk = ((z + distance + RING) % RING) * GROUP

        def store(c, _):
            for half in range(2):
                p = order[2 * (chunk + c) + half]
                dkv[chunk + c, 0, half] = (dk[p] * SCALE).astype(BF)
                dkv[chunk + c, 1, half] = (dv[p] * 2.0).astype(BF)
            return 0

        lax.fori_loop(0, GROUP, store, 0)

    reducing = {}

    def reduce(step, part):
        for lane, way in enumerate((1, -1)):
            chunk = ((z + way * (RING // 2 - step) + RING) % RING) * GROUP
            mine = pl.ds(chunk + chips[part], 2)
            if step > 0:
                reducing[lane, part].wait_recv()
                terms = dkv[mine].astype(F32)
                partial = sums.at[lane, step - 1, part]
            if step == 0:
                source, target = dkv.at[mine, :, lane], landed_half.at[lane, part]
            else:
                if step == 1:
                    arrived = landed_half[lane, part].astype(F32)
                    partial[:, :, lane] = (terms[:, :, lane] + arrived).astype(BF)
                    partial[:, :, 1 - lane] = dkv[mine, :, 1 - lane]
                else:
                    arrived = landed[lane, step - 2, part].astype(F32)
                    partial[...] = (terms + arrived).astype(BF)
                source, target = partial, landed.at[lane, step - 1, part]
            copy = remote(
                source, target, r_send.at[lane], r_recv.at[lane, step, part],
                ctx_of(z + way, m),
            )
            copy.start()
            reducing[lane, part] = copy

    store_chunk(RING // 2)
    reduce(0, 1)
    reduce(0, 0)
    for distance in (3, -3):
        store_chunk(distance)
    for i in range(GROUP):
        put_rows(
            dq, i, (acc_t[0, :, span[i]] * SCALE).T, (acc_t[1, :, span[i]] * SCALE).T
        )
    dq_copies = exchange(5, dq, dq_in, m)
    dq_in[m] = dq[m]
    for distance in (2, -2, 1, -1, 0):
        store_chunk(distance)


    gathered(0)
    arrive(qf_copies)
    unsort(in_kvf)
    for i in range(GROUP):
        for w in range(2):
            qs[w, i] = query_rows(in_qf, i, w)
    query_over = lax.broadcasted_iota(jnp.int32, (QROWS, BLOCK), 1) - (
        lax.broadcasted_iota(jnp.int32, (QROWS, BLOCK), 0) % HALF
    )

    def weigh(q, k):
        u = dot_nt(q, k) * (0.5 * SCALE)
        return u + u * jnp.tanh(u)

    def forward_full(part):
        pairs = slice(2 * part, 2 * part + 2)
        rows = slice(2 * part * QROWS, 2 * (part + 1) * QROWS)

        def step(b, _):
            q = qs[1, pairs].reshape(2 * QROWS, HEAD)
            acc[1, rows] += dot_nn(weigh(q, ks[b]).astype(BF), vs[b])
            return 0

        lax.fori_loop(0, half_blocks, step, 0)

    def forward_edge(part):
        for i in (2 * part, 2 * part + 1):
            at = last - quart[i]
            p = seen(query_over, bound_high(i), weigh(qs[1, i], ks[at]))
            acc[1, span[i]] += dot_nn(p, vs[at])

    def forward_choice(part, first, end):
        def step(n, _):
            for i in (2 * part, 2 * part + 1):
                is_low, at, w = choice(i, n)
                p = seen(query_over, bound_low(i, n), weigh(qs[w, i], ks[at]))
                out = dot_nn(p, vs[at])
                acc[0, span[i]] += jnp.where(is_low, out, 0.0)
                acc[1, span[i]] += jnp.where(is_low, 0.0, out)
            return 0

        lax.fori_loop(first, end, step, 0)


    norm_copies = [[], []]

    def measure_rows(part):
        for i in (2 * part, 2 * part + 1):
            shape = (4, HALF, HEAD)
            low_rows = (acc[0, span[i]] * shrink_rows(stretch[0][i])).reshape(shape)
            high_rows = (acc[1, span[i]] * shrink_rows(stretch[1][i])).reshape(shape)
            att[i, 0] = jnp.where(low_half[i] == 0, low_rows, high_rows)
            att[i, 1] = jnp.where(low_half[i] == 0, high_rows, low_rows)
            rows = att[i]
            square = jnp.sum(rows * rows, axis=1).reshape(ROWS, HEAD)
            square = jnp.sum(square, axis=1, keepdims=True)
            norms[i] = jnp.broadcast_to(square, (ROWS, HEAD)).T[:8]
        pairs = pl.ds(2 * part, 2)
        for d, p in enumerate(peers):
            copy = remote(
                norms.at[pairs], norms_in.at[d, pairs],
                n_send, n_recv.at[d, part], ctx_of(z, p),
            )
            copy.start()
            norm_copies[part].append(copy)

    def hand_rows(part):
        arrive(norm_copies[part])
        for i in (2 * part, 2 * part + 1):
            row = norms[i] + norms_in[0, i] + norms_in[1, i] + norms_in[2, i]
            square = jnp.broadcast_to(row[:1], (HEAD, ROWS)).T
            factor = lax.rsqrt(square * (1.0 / (16 * HEAD)) + EPS).reshape(2, 1, HALF, HEAD)
            for g in range(4):
                cols = pl.ds(pl.multiple_of((m * 4 + g) * HEAD, HEAD), HEAD)
                gated[i, :, g] = (
                    att[i, :, g] * factor[:, 0]
                    * gain[:, cols].reshape(1, 1, HEAD)
                    * in_gate[i, :, g].astype(F32)
                ).astype(BF)
            copy = remote(
                gated.at[i], hand_in.at[m], h_send, h_recv.at[m], beside(1, i)
            )
            copy.start()

    acc[...] = jnp.zeros_like(acc)
    forward_full(0)
    reduce(1, 1)
    reduce(1, 0)
    forward_edge(0)
    forward_choice(0, 0, half_blocks)
    measure_rows(0)
    reduce(2, 1)
    forward_full(1)
    reduce(2, 0)
    arrive(gate_copies)
    hand_rows(0)
    forward_edge(1)
    forward_choice(1, 0, half_blocks)
    measure_rows(1)
    reduce(3, 1)
    hand_rows(1)
    reduce(3, 0)
    arrive(dq_copies)
    for h in range(GROUP):
        for g in range(4):
            for half in range(2):
                rows = slice(half * HALF, (half + 1) * HALF)
                query_grad[rows, columns(h * 4 + g)] = dq_in[h, half, g]


    for part in (1, 0):
        for lane in range(2):
            reducing[lane, part].wait_recv()
        total[pl.ds(chips[part], 2)] = (
            dkv[pl.ds(z * GROUP + chips[part], 2)].astype(F32)
            + landed[0, RING // 2 - 2, part].astype(F32)
            + landed[1, RING // 2 - 2, part].astype(F32)
        ).astype(BF)
        for d in ((1, 2), (0,))[1 - part]:
            copy = remote(
                total.at[peers[d]], dkv_in.at[m], a_send.at[7], a_recv.at[d, 7],
                ctx_of(z, peers[d]),
            )
            copy.start()
            moving[2, 0, d] = copy
    dkv_in[m] = total[m]
    gathered(2)
    for h in range(GROUP):
        for half in range(2):
            rows = slice(half * HALF, (half + 1) * HALF)
            key_grad[rows, columns(h)] = dkv_in[h, 0, half]
            value_grad[rows, columns(h)] = dkv_in[h, 1, half]
    for h in range(GROUP):
        remote(gated.at[h], hand_in.at[h], h_send, h_recv.at[h], beside(1, h)).wait_recv()
        for g in range(4):
            for half in range(2):
                rows = slice(half * HALF, (half + 1) * HALF)
                handed[rows, columns(h * 4 + g)] = hand_in[h, half, g]
    ring = pl.ds(0, GROUP * RING // 2 - 2)
    for lane in range(2):
        sent.append((in_kvb.at[ring], b_send.at[lane]))
        sent.append((in_kvf.at[ring], g_send.at[lane]))
        sent.append((dkv.at[ring], r_send.at[lane]))
    sent.append((total.at[pl.ds(0, len(peers))], a_send.at[7]))
    sent.append((norms_in, n_send))
    sent.append((gated, h_send))
    for view, send in sent:
        remote(view, view, send, h_recv.at[0], ctx_of(z, peers[0])).wait_send()


def copy_kernel(*refs):
    for source, target in zip(refs[:4], refs[4:], strict=True):
        target[...] = source[...]


def body(
    query_fwd, key_fwd, value_fwd, gate_fwd, types_fwd,
    query_bwd, key_bwd, value_bwd, grad_out, types_bwd,
    type_key, norm_gain, stretch_order,
):
    order = stretch_order[0]
    dma = pltpu.SemaphoreType.DMA
    wide, narrow = (ROWS, 16 * HEAD), (ROWS, GROUP * HEAD)
    smem = pl.BlockSpec(memory_space=pltpu.SMEM)
    part = (HALF, HEAD)
    blocks = TOKENS // BLOCK
    heads, pairs = (GROUP, 2, 4, *part), (CTX, 2, 2, *part)
    handed, query_grad, key_grad, value_grad = pl.pallas_call(
        kernel,
        out_shape=(
            jax.ShapeDtypeStruct(wide, BF),
            jax.ShapeDtypeStruct(wide, BF),
            jax.ShapeDtypeStruct(narrow, BF),
            jax.ShapeDtypeStruct(narrow, BF),
        ),
        in_specs=[smem] + [VMEM] * 6 + [pl.BlockSpec(memory_space=pl.ANY)] * 6,
        out_specs=(VMEM,) * 4,
        scratch_shapes=[
            pltpu.SMEM((2 * CTX,), jnp.int32),
            pltpu.VMEM((4, *heads), BF),
            pltpu.VMEM((2, GROUP, 2, 2, *part), BF),
            pltpu.VMEM(heads, BF),
            pltpu.VMEM(heads, BF),
            pltpu.VMEM(heads, BF),
            pltpu.VMEM(heads, BF),
            pltpu.VMEM(pairs, BF),
            pltpu.VMEM(pairs, BF),
            pltpu.VMEM((blocks, BLOCK, HEAD), BF),
            pltpu.VMEM((blocks, BLOCK, HEAD), BF),
            pltpu.VMEM((blocks, HEAD, BLOCK), BF),
            pltpu.VMEM((2 * CTX, *part), F32),
            pltpu.VMEM((2 * CTX, *part), F32),
            pltpu.VMEM((2, GROUP * QROWS, HEAD), F32),
            pltpu.VMEM((2, HEAD, GROUP * QROWS), F32),
            pltpu.VMEM((2, GROUP, QROWS, HEAD), BF),
            pltpu.VMEM((2, GROUP, QROWS, HEAD), BF),
            pltpu.VMEM((2, HEAD, GROUP * QROWS), BF),
            pltpu.VMEM((2, HEAD, GROUP * QROWS), BF),
            pltpu.VMEM((GROUP, BLOCK, HEAD), F32),
            pltpu.VMEM((GROUP, BLOCK, HEAD), F32),
            pltpu.VMEM((2, GROUP, QROWS, 2 * HEAD), BF),
            pltpu.VMEM((2, GROUP, QROWS, 2 * HEAD), BF),
            pltpu.VMEM(pairs, BF),
            pltpu.VMEM((2, RING // 2 - 1, 2, 2, 2, 2, *part), BF),
            pltpu.VMEM((2, RING // 2 - 1, 2, 2, 2, 2, *part), BF),
            pltpu.VMEM((2, 2, 2, 2, *part), BF),
            pltpu.VMEM((GROUP, 2, 2, *part), BF),
            pltpu.VMEM((GROUP, 2, 2, *part), BF),
            pltpu.VMEM(heads, F32),
            pltpu.VMEM((GROUP, 8, ROWS), F32),
            pltpu.VMEM((3, GROUP, 8, ROWS), F32),
            pltpu.VMEM(heads, BF),
            pltpu.VMEM(heads, BF),
            pltpu.VMEM(heads, BF),
            pltpu.VMEM(heads, BF),
            dma((8,)),
            dma((3, 8)),
            dma((2,)),
            dma((2, RING // 2, GROUP)),
            dma((2,)),
            dma((2, RING // 2, 2)),
            dma((2,)),
            dma((2, RING // 2, 2)),
            dma,
            dma((3, 2)),
            dma,
            dma((GROUP,)),
            pltpu.VMEM(wide, BF),
            pltpu.VMEM(wide, BF),
            pltpu.VMEM(narrow, BF),
            pltpu.VMEM(narrow, BF),
            pltpu.VMEM(wide, BF),
            pltpu.VMEM(wide, BF),
            dma((6,)),
        ],
        compiler_params=pltpu.CompilerParams(
            collective_id=0, has_side_effects=True, vmem_limit_bytes=56 * 1024 * 1024
        ),
        name="attention",
    )(
        order, types_fwd, types_bwd, type_key[0], key_bwd[0], value_bwd[0], norm_gain,
        query_bwd[0], grad_out[0], key_fwd[0], value_fwd[0], query_fwd[0], gate_fwd[0],
    )
    outs = (handed, query_grad, key_grad, value_grad)
    outs = pl.pallas_call(
        copy_kernel,
        out_shape=tuple(jax.ShapeDtypeStruct(o.shape, o.dtype) for o in outs),
        in_specs=[VMEM] * 4,
        out_specs=(VMEM,) * 4,
        name="finish",
    )(*outs)
    return tuple(o[None] for o in outs)


def solution(mesh):
    rows = P("pipe", "ctx", None)
    section = P("pipe", None)
    types = P("pipe", "ctx")
    return jax.shard_map(
        body,
        mesh=mesh,
        in_specs=(
            rows, rows, rows, rows, types, rows, rows, rows, rows, types,
            P("pipe", None, None), section, section,
        ),
        out_specs=(rows, rows, rows, rows),
        check_vma=False,
    )
```
